32 devices in a mesh: tm: 4 (over z), docs: 8 (over y, x, core).
Axes of the slice: x: 2, y: 2, z: 4, core: 2. Of those that a mesh axis runs over, the one named last changes fastest.
Arguments:
- counts: int32 [4, 512, 32768], P('tm', 'docs'), may hold values from 0 to 5, as said below
- topic_means: float32 [4, 32768, 128], P('tm', 'docs'), may hold values from -80 to 170
- doc_topics_init: float32 [4, 512, 128], P('tm', 'docs'), may hold values from 0.5 to 20
- dirichlet_prior: float32 [128], replicated, may hold values from 0.05 to 1
- chain_var: float32 [128], replicated, may hold values from 0.005 to 0.5
- obs_noise: float32 [128], replicated, may hold values from 0.1 to 10
Outputs:
- smoothed_means: float32 [4, 32768, 128], P('tm', 'docs')
- doc_topics: float32 [4, 512, 128], P('tm', 'docs')
The draws below stay inside these ranges and needn't reach their ends.
Inputs may be any that keep to these rules, and one draw needn't show every extreme that they name: `counts`: each entry is 0 or a count of 1 to 5; each word has its own share of nonzero entries, between a quarter and three quarters.
All inputs are finite; a program needn't handle non-finite values.
Results may differ from the reference program's by a relative error of at most 0.01.
Values may be sent and summed in bfloat16 or wider, within the bound.
A program may use at most 128 MiB of HBM per device.

```python
import math
import jax
import jax.numpy as jnp
from jax import lax

V = 32768
K = 128
ITERS_E = 4
SLICES = 4
DOCS_ALL = 512


def draw_counts(key, part):
    chance_key, value_key, density_key = jax.random.split(key, 3)
    density = jax.random.randint(density_key, (V,), 16, 49)
    chance = jax.random.randint(chance_key, (SLICES, DOCS_ALL, V), 0, 64)
    values = jax.random.randint(value_key, (SLICES, DOCS_ALL, V), 1, 6)
    return jnp.where(chance < density[None, None, :], values, 0).astype(jnp.int32)


def draw_topic_means(key, part):
    streams = jax.random.split(key, 2)
    rough_part = 1.5 * jnp.clip(jax.random.normal(streams[0], (SLICES, V, K), jnp.float32), -4.0, 4.0)
    offset = jax.random.uniform(streams[1], (SLICES, 1, K), jnp.float32, -2.0, 2.0)
    return (rough_part + offset).astype(jnp.float32)


def steps_of(stream_key, extent, cuts, smallest, top_value):
    level, own = 1.0, jax.random.fold_in(stream_key, 6)
    for position, parts in cuts:
        heights = jnp.exp(jax.random.uniform(jax.random.fold_in(own, position), (parts,), jnp.float32, smallest / len(cuts), top_value / len(cuts)))
        level = level * jnp.repeat(heights, extent[position] // parts).reshape([-1 if axis == position else 1 for axis in range(len(extent))])
    return level


def setup_inputs(seed: int = 0) -> dict:
    seeds = jax.random.split(jax.random.key(seed), 7)
    counts = draw_counts(jax.random.fold_in(seeds[6], 71), 0)
    topic_means = draw_topic_means(jax.random.fold_in(seeds[6], 71), 0)
    doc_topics_init = jnp.clip(jnp.exp(math.log(20.0) - 3.6888795 * jax.random.uniform(seeds[2], (SLICES, DOCS_ALL, K), jnp.float32) ** steps_of(seeds[2], (SLICES, DOCS_ALL, K), ((0, 4), (1, 8)), -0.2, 0.2)), 0.5, 20.0)
    dirichlet_prior = jnp.clip(jnp.exp(jax.random.uniform(seeds[3], (K,), jnp.float32, math.log(0.05), math.log(1.0))), 0.05, 1.0)
    chain_var = jnp.clip(jnp.exp(jax.random.uniform(seeds[4], (K,), jnp.float32, math.log(0.005), math.log(0.5))), 0.005, 0.5)
    obs_noise = jnp.clip(jnp.exp(jax.random.uniform(seeds[5], (K,), jnp.float32, math.log(0.1), math.log(10.0))), 0.1, 10.0)
    return dict(counts=counts, topic_means=topic_means, doc_topics_init=doc_topics_init, dirichlet_prior=dirichlet_prior, chain_var=chain_var, obs_noise=obs_noise)


prior_count = 0.5
initial_scale = 1000.0


def chain_factors(totals, chain_var, obs_noise):
    relative = jnp.sum(totals, axis=1, keepdims=True) / (totals.shape[1] * totals)
    noise = obs_noise[None, :] * relative

    def advance(previous, noise_level):
        predicted = previous + chain_var
        own_gain = predicted / (predicted + noise_level)
        current = (1.0 - own_gain) * predicted
        return current, (own_gain, current)

    unused, (gains, filtered_var) = lax.scan(advance, initial_scale * chain_var, noise)
    smooth = filtered_var / (filtered_var + chain_var)
    smooth = jnp.concatenate([smooth[:-1], jnp.zeros_like(smooth[-1:])], axis=0)
    return gains, smooth


def reference(counts, topic_means, doc_topics_init, dirichlet_prior, chain_var, obs_noise):
    def one_slice(inputs):
        count_rows, slab_means, concentration = inputs
        beta = jax.nn.softmax(slab_means, axis=0).astype(jnp.bfloat16)
        beta_wide = beta.astype(jnp.float32)
        count_wide = count_rows.astype(jnp.float32)
        for sweep_index in range(ITERS_E):
            proportions = jnp.exp(lax.digamma(concentration)).astype(jnp.bfloat16)
            theta_wide = proportions.astype(jnp.float32)
            mixture = jnp.dot(theta_wide, beta_wide.T, preferred_element_type=jnp.float32)
            ratios = (count_wide / mixture).astype(jnp.bfloat16)
            ratio_wide = ratios.astype(jnp.float32)
            update = theta_wide * jnp.dot(ratio_wide, beta_wide, preferred_element_type=jnp.float32)
            concentration = dirichlet_prior[None, :] + update
        word_stats = beta_wide * jnp.dot(ratio_wide.T, theta_wide, preferred_element_type=jnp.float32)
        return word_stats, concentration, jnp.sum(update, axis=0)

    word_stats, doc_topics, totals = lax.map(one_slice, (counts, topic_means, doc_topics_init))
    gains, smooth = chain_factors(totals, chain_var, obs_noise)
    pseudo = jnp.log(word_stats + prior_count) - jnp.log((totals[:, None, :] + prior_count * V) / V)

    def forward(previous, inputs):
        own_gain, observed = inputs
        current = (1.0 - own_gain) * previous + own_gain * observed
        return current, current

    unused, filtered = lax.scan(forward, jnp.zeros_like(pseudo[0]), (gains[:, None, :], pseudo))

    def backward(following, inputs):
        factor, current = inputs
        result = (1.0 - factor) * current + factor * following
        return result, result

    unused, smoothed = lax.scan(backward, jnp.zeros_like(pseudo[0]), (smooth[:, None, :], filtered), reverse=True)
    return smoothed, doc_topics
```

```python
import functools

import jax
import jax.numpy as jnp
from jax import lax
from jax.experimental import pallas as pl
from jax.experimental.pallas import tpu as pltpu
from jax.sharding import PartitionSpec as P

ITERS_E = 4
prior_count = 0.5
initial_scale = 1000.0
MESH = pl.DeviceIdType.MESH
BF = jnp.bfloat16
F32 = jnp.float32


def expected_proportions(x):
    u = x * (x + 5.0)
    steps = (2.0 * x + 5.0) * (1.0 / u + 1.0 / (u + 4.0) + 1.0 / (u + 6.0))
    y = x + 6.0
    inv = 1.0 / y
    sq = inv * inv
    tail = sq * (1.0 / 12 - sq * (1.0 / 120 - sq * (1.0 / 252 - sq * (1.0 / 240))))
    return jnp.exp(jnp.log(y) - 0.5 * inv - tail - steps)


def round_kernel(n, slices, word_tile, chunk, counts_ref, slab_ref, init_ref, prior_ref, chain_ref,
                 obs_ref, smooth_ref, topics_ref, raw, outgoing, ratio, weights, beta, theta,
                 acc, part_out, part_in, stat_out, stat_in, tot_out, tot_in, row_out, row_in,
                 fwd_in, back_in, fwd_out, back_out, load_sem, cnt_s, cnt_r, theta_s, theta_r,
                 part_s, part_r, stat_s, stat_r, tot_s, tot_r, row_s, row_r, fwd_s, fwd_r,
                 back_s, back_r):
    docs = init_ref.shape[0]
    words = slab_ref.shape[0]
    me = lax.axis_index("docs")
    now = lax.axis_index("tm")

    def peers(fn, size, own):
        def step(m, carry):
            fn(lax.rem(own + m, size))
            return carry
        lax.fori_loop(1, size, step, 0)

    def rows(p):
        return pl.ds(pl.multiple_of(p * docs, docs), docs)

    def load(p):
        return pltpu.make_async_copy(
            counts_ref.at[:, pl.ds(pl.multiple_of(p * words, words), words)], raw.at[p],
            load_sem.at[p])

    def to_docs(src, dst, s, r, p):
        return pltpu.make_async_remote_copy(src_ref=src, dst_ref=dst, send_sem=s, recv_sem=r,
                                            device_id={"docs": p}, device_id_type=MESH)

    def to_tm(src, dst, s, r, p):
        return pltpu.make_async_remote_copy(src_ref=src, dst_ref=dst, send_sem=s, recv_sem=r,
                                            device_id={"tm": p}, device_id_type=MESH)

    def load_all(p, carry):
        load(p).start()
        return carry

    lax.fori_loop(0, n, load_all, 0)

    barrier = pltpu.get_barrier_semaphore()
    peers(lambda p: pl.semaphore_signal(barrier, inc=1, device_id={"docs": p},
                                        device_id_type=MESH), n, me)
    peers(lambda p: pl.semaphore_signal(barrier, inc=1, device_id={"tm": p},
                                        device_id_type=MESH), slices, now)

    first = expected_proportions(init_ref[...]).astype(BF)
    theta[0, rows(me), :] = first
    peak = jnp.max(slab_ref[...], axis=0, keepdims=True)
    weights[...] = jnp.exp(slab_ref[...] - peak)
    mass = jnp.sum(weights[...], axis=0, keepdims=True)
    eight = (8, peak.shape[1])
    stat_out[0] = jnp.broadcast_to(peak, eight)
    stat_out[1] = jnp.broadcast_to(mass, eight)
    pl.semaphore_wait(barrier, n - 1 + slices - 1)

    def theta_copy(it, src_block, p, r):
        block = theta.at[it, rows(src_block), :]
        return to_docs(block, block, theta_s.at[it, p], theta_r.at[it, r], p)

    def stat_copy(src_block, p):
        return to_docs(stat_out, stat_in.at[src_block], stat_s.at[p], stat_r.at[src_block], p)

    def cnt_copy(src_block, p):
        return to_docs(outgoing.at[p], ratio.at[rows(src_block), :], cnt_s.at[p],
                       cnt_r.at[src_block], p)

    def part_copy(it, src_block, p):
        return to_docs(part_out.at[it, rows(p), :], part_in.at[it, src_block],
                       part_s.at[it, p], part_r.at[it, src_block], p)

    def tot_copy(src_block, p):
        return to_docs(tot_out, tot_in.at[src_block], tot_s.at[p], tot_r.at[src_block], p)

    def row_copy(src_block, p):
        return to_tm(row_out, row_in.at[src_block], row_s.at[p], row_r.at[src_block], p)

    peers(lambda p: stat_copy(me, p).start(), n, me)
    peers(lambda p: theta_copy(0, me, p, me).start(), n, me)

    def send_counts(p):
        load(p).wait()
        outgoing[p] = raw[p].astype(F32).astype(BF)
        cnt_copy(me, p).start()

    peers(send_counts, n, me)
    load(me).wait()
    ratio[rows(me), :] = raw[me].astype(F32).astype(BF)

    stat_in[me] = stat_out[...]
    peers(lambda q: stat_copy(q, q).wait_recv(), n, me)
    all_peaks = [stat_in[q, 0, 0:1, :] for q in range(n)]
    top = functools.reduce(jnp.maximum, all_peaks)
    total_mass = sum(stat_in[q, 1, 0:1, :] * jnp.exp(all_peaks[q] - top) for q in range(n))
    beta[...] = (weights[...] * (jnp.exp(peak - top) / total_mass)).astype(BF)

    peers(lambda q: theta_copy(0, q, q, q).wait_recv(), n, me)
    peers(lambda q: cnt_copy(q, q).wait_recv(), n, me)

    prior = prior_ref[...]
    for it in range(ITERS_E):
        last = it == ITERS_E - 1
        acc[...] = jnp.zeros_like(acc)

        def sweep_tile(i, carry):
            cols = pl.ds(pl.multiple_of(i * word_tile, word_tile), word_tile)
            tile = beta[cols, :]
            mixture = lax.dot_general(theta[it], tile, (((1,), (1,)), ((), ())),
                                      preferred_element_type=F32)
            quotient = (ratio[:, cols].astype(F32) / mixture).astype(BF)
            if last:
                ratio[:, cols] = quotient
            acc[...] += jnp.dot(quotient, tile, preferred_element_type=F32)
            return carry

        lax.fori_loop(0, words // word_tile, sweep_tile, 0)
        if last:
            own = jnp.sum(theta[it].astype(F32) * acc[...], axis=0, keepdims=True)
            tot_out[...] = jnp.broadcast_to(own, eight)
            peers(lambda p: tot_copy(me, p).start(), n, me)
        part_out[it] = acc[...].astype(BF)
        peers(lambda p: part_copy(it, me, p).start(), n, me)
        if last:
            def stats_tile(i, carry):
                cols = pl.ds(pl.multiple_of(i * word_tile, word_tile), word_tile)
                gathered = lax.dot_general(ratio[:, cols], theta[it], (((0,), (0,)), ((), ())),
                                           preferred_element_type=F32)
                weights[cols, :] = jnp.log(beta[cols, :].astype(F32) * gathered + prior_count)
                return carry

            half = words // word_tile // 2
            lax.fori_loop(0, half, stats_tile, 0)
            tot_in[me] = tot_out[...]
            peers(lambda q: tot_copy(q, q).wait_recv(), n, me)
            row_out[...] = sum(tot_in[q] for q in range(n))
            peers(lambda p: row_copy(now, p).start(), slices, now)
            lax.fori_loop(half, words // word_tile, stats_tile, 0)
        part_in[it, me] = part_out[it, rows(me), :]
        peers(lambda q: part_copy(it, q, q).wait_recv(), n, me)
        summed = sum(part_in[it, q].astype(F32) for q in range(n))
        gamma = prior + theta[it, rows(me), :].astype(F32) * summed
        if last:
            topics_ref[...] = gamma
        else:
            theta[it + 1, rows(me), :] = expected_proportions(gamma).astype(BF)
            peers(lambda p: theta_copy(it + 1, me, p, me).start(), n, me)
            peers(lambda q: theta_copy(it + 1, q, q, q).wait_recv(), n, me)

    row_in[now] = row_out[...]
    peers(lambda q: row_copy(q, q).wait_recv(), slices, now)

    chain = chain_ref[...]
    topics = chain.shape[1]
    previous = initial_scale * chain
    gains, factors = [], []
    for t in range(slices):
        totals = row_in[t, 0:1, :]
        noise = obs_ref[...] * (jnp.sum(totals, axis=1, keepdims=True) / (topics * totals))
        predicted = previous + chain
        gain = predicted / (predicted + noise)
        previous = (1.0 - gain) * predicted
        gains.append(gain)
        factors.append(previous / (previous + chain) if t < slices - 1 else jnp.zeros_like(chain))
    share = [None] * slices
    share[-1] = jnp.ones_like(chain)
    for t in range(slices - 2, -1, -1):
        share[t] = (1.0 - factors[t]) + factors[t] * (1.0 - gains[t + 1]) * share[t + 1]

    def mine(per_slice):
        value = per_slice[0]
        for t in range(1, slices):
            value = jnp.where(now == t, per_slice[t], value)
        return value

    gain, factor, left = mine(gains), mine(factors), mine(share)
    all_words = words * n
    offset = jnp.log((row_in[now, 0:1, :] + prior_count * all_words) / all_words)
    keep = 1.0 - gain
    carried = left * keep
    direct = left * gain

    @pl.when(now == 0)
    def _():
        fwd_in[...] = jnp.zeros_like(fwd_in)

    @pl.when(now == slices - 1)
    def _():
        back_in[...] = jnp.zeros_like(back_in)

    pieces = words // chunk

    def piece(i):
        return pl.ds(pl.multiple_of(i * chunk, chunk), chunk)

    def fwd_copy(i):
        return to_tm(fwd_out.at[piece(i), :], fwd_in.at[piece(i), :], fwd_s.at[i], fwd_r.at[i],
                     lax.rem(now + 1, slices))

    def back_copy(i):
        return to_tm(back_out.at[piece(i), :], back_in.at[piece(i), :], back_s.at[i],
                     back_r.at[i], lax.rem(now + slices - 1, slices))

    lag = slices - 1 - 2 * now
    fwd_lag = jnp.maximum(-lag, 0)
    back_lag = jnp.maximum(lag, 0)
    both_lag = jnp.maximum(fwd_lag, back_lag)

    def step(i, carry):
        f, b, s = i - fwd_lag, i - back_lag, i - both_lag

        @pl.when((f >= 0) & (f < pieces))
        def _():
            @pl.when(now > 0)
            def _():
                fwd_copy(f).wait_recv()

            @pl.when(now < slices - 1)
            def _():
                at = piece(f)
                observed = weights[at, :] - offset
                fwd_out[at, :] = (keep * fwd_in[at, :].astype(F32) + gain * observed).astype(BF)
                fwd_copy(f).start()

        @pl.when((b >= 0) & (b < pieces))
        def _():
            @pl.when(now < slices - 1)
            def _():
                back_copy(b).wait_recv()

            @pl.when(now > 0)
            def _():
                at = piece(b)
                observed = weights[at, :] - offset
                back_out[at, :] = (factor * back_in[at, :].astype(F32)
                                   + direct * observed).astype(BF)
                back_copy(b).start()

        @pl.when((s >= 0) & (s < pieces))
        def _():
            at = piece(s)
            smooth_ref[at, :] = (carried * fwd_in[at, :].astype(F32)
                                 + direct * (weights[at, :] - offset)
                                 + factor * back_in[at, :].astype(F32))
        return carry

    lax.fori_loop(0, pieces + slices - 1, step, 0)

    peers(lambda p: stat_copy(me, p).wait_send(), n, me)
    peers(lambda p: cnt_copy(me, p).wait_send(), n, me)
    peers(lambda p: tot_copy(me, p).wait_send(), n, me)
    peers(lambda p: row_copy(now, p).wait_send(), slices, now)
    for it in range(ITERS_E):
        peers(lambda p: theta_copy(it, me, p, me).wait_send(), n, me)
        peers(lambda p: part_copy(it, me, p).wait_send(), n, me)

    def drain(i, carry):
        @pl.when(now < slices - 1)
        def _():
            fwd_copy(i).wait_send()

        @pl.when(now > 0)
        def _():
            back_copy(i).wait_send()
        return carry

    lax.fori_loop(0, pieces, drain, 0)


def body(counts, topic_means, doc_topics_init, dirichlet_prior, chain_var, obs_noise):
    n = lax.axis_size("docs")
    slices = lax.axis_size("tm")
    docs = counts.shape[1]
    words, topics = topic_means.shape[1:]
    every = docs * n
    word_tile = min(512, words // 2)
    chunk = max(words // 8, 16)
    pieces = words // chunk
    dma = pltpu.SemaphoreType.DMA
    vmem = pl.BlockSpec(memory_space=pltpu.VMEM)
    smoothed, doc_topics = pl.pallas_call(
        functools.partial(round_kernel, n, slices, word_tile, chunk),
        out_shape=(jax.ShapeDtypeStruct((words, topics), F32),
                   jax.ShapeDtypeStruct((docs, topics), F32)),
        in_specs=[pl.BlockSpec(memory_space=pl.ANY)] + [vmem] * 5,
        out_specs=(vmem, vmem),
        scratch_shapes=[
            pltpu.VMEM((n, docs, words), jnp.int32),
            pltpu.VMEM((n, docs, words), BF),
            pltpu.VMEM((every, words), BF),
            pltpu.VMEM((words, topics), F32),
            pltpu.VMEM((words, topics), BF),
            pltpu.VMEM((ITERS_E, every, topics), BF),
            pltpu.VMEM((every, topics), F32),
            pltpu.VMEM((ITERS_E, every, topics), BF),
            pltpu.VMEM((ITERS_E, n, docs, topics), BF),
            pltpu.VMEM((2, 8, topics), F32),
            pltpu.VMEM((n, 2, 8, topics), F32),
            pltpu.VMEM((8, topics), F32),
            pltpu.VMEM((n, 8, topics), F32),
            pltpu.VMEM((8, topics), F32),
            pltpu.VMEM((slices, 8, topics), F32),
            pltpu.VMEM((words, topics), BF),
            pltpu.VMEM((words, topics), BF),
            pltpu.VMEM((words, topics), BF),
            pltpu.VMEM((words, topics), BF),
            dma((n,)),
            dma((n,)), dma((n,)),
            dma((ITERS_E, n)), dma((ITERS_E, n)),
            dma((ITERS_E, n)), dma((ITERS_E, n)),
            dma((n,)), dma((n,)),
            dma((n,)), dma((n,)),
            dma((slices,)), dma((slices,)),
            dma((pieces,)), dma((pieces,)),
            dma((pieces,)), dma((pieces,)),
        ],
        compiler_params=pltpu.CompilerParams(
            collective_id=0, has_side_effects=True, vmem_limit_bytes=58 * 1024 * 1024),
    )(counts[0], topic_means[0], doc_topics_init[0], dirichlet_prior[None], chain_var[None],
      obs_noise[None])
    return smoothed[None], doc_topics[None]


def solution(mesh):
    in_specs = (P("tm", "docs", None), P("tm", "docs", None), P("tm", "docs", None), P(), P(), P())
    out_specs = (P("tm", "docs", None), P("tm", "docs", None))
    return jax.shard_map(body, mesh=mesh, in_specs=in_specs, out_specs=out_specs, check_vma=False)
```

```python
import functools

import jax
import jax.numpy as jnp
from jax import lax
from jax.experimental import pallas as pl
from jax.experimental.pallas import tpu as pltpu
from jax.sharding import PartitionSpec as P

ITERS_E = 4
prior_count = 0.5
initial_scale = 1000.0
MESH = pl.DeviceIdType.MESH
BF = jnp.bfloat16
F32 = jnp.float32


def expected_proportions(x):
    u = x * (x + 5.0)
    steps = (2.0 * x + 5.0) * (1.0 / u + 1.0 / (u + 4.0) + 1.0 / (u + 6.0))
    y = x + 6.0
    inv = 1.0 / y
    sq = inv * inv
    tail = sq * (1.0 / 12 - sq * (1.0 / 120 - sq * (1.0 / 252 - sq * (1.0 / 240))))
    return jnp.exp(jnp.log(y) - 0.5 * inv - tail - steps)


def round_kernel(n, slices, word_tile, chunk, sizes, plan, counts_ref, slab_ref, init_ref, prior_ref, chain_ref,
                 obs_ref, smooth_ref, topics_ref, raw, outgoing, ratio, weights, beta, theta,
                 acc, part_out, part_in, stat_out, stat_in, tot_out, tot_in, row_out, row_in,
                 fwd_in, back_in, fwd_out, back_out, load_sem, cnt_s, cnt_r, theta_s, theta_r,
                 part_s, part_r, stat_s, stat_r, tot_s, tot_r, row_s, row_r, fwd_s, fwd_r,
                 back_s, back_r):
    docs = init_ref.shape[0]
    words = slab_ref.shape[0]
    me = lax.axis_index("docs")
    now = lax.axis_index("tm")

    def peers(fn, size, own):
        def step(m, carry):
            fn(lax.rem(own + m, size))
            return carry
        lax.fori_loop(1, size, step, 0)

    starts = [sum(sizes[:g]) for g in range(len(sizes))]

    def rows(g, p):
        return pl.ds(pl.multiple_of(starts[g] * n + p * sizes[g], 16), sizes[g])

    def members(g):
        return pl.ds(starts[g] * n, sizes[g] * n)

    def inner(g):
        return pl.ds(starts[g], sizes[g])

    def load(p):
        return pltpu.make_async_copy(
            counts_ref.at[:, pl.ds(pl.multiple_of(p * words, words), words)], raw.at[p],
            load_sem.at[p])

    def to_docs(src, dst, s, r, p):
        return pltpu.make_async_remote_copy(src_ref=src, dst_ref=dst, send_sem=s, recv_sem=r,
                                            device_id={"docs": p}, device_id_type=MESH)

    def to_tm(src, dst, s, r, p):
        return pltpu.make_async_remote_copy(src_ref=src, dst_ref=dst, send_sem=s, recv_sem=r,
                                            device_id={"tm": p}, device_id_type=MESH)

    def load_all(p, carry):
        load(p).start()
        return carry

    lax.fori_loop(0, n, load_all, 0)

    barrier = pltpu.get_barrier_semaphore()
    peers(lambda p: pl.semaphore_signal(barrier, inc=1, device_id={"docs": p},
                                        device_id_type=MESH), n, me)
    peers(lambda p: pl.semaphore_signal(barrier, inc=1, device_id={"tm": p},
                                        device_id_type=MESH), slices, now)

    def theta_copy(g, it, src_block, p, r):
        block = theta.at[it, rows(g, src_block), :]
        return to_docs(block, block, theta_s.at[g, it, p], theta_r.at[g, it, r], p)

    def stat_copy(src_block, p):
        return to_docs(stat_out, stat_in.at[src_block], stat_s.at[p], stat_r.at[src_block], p)

    def cnt_copy(g, src_block, p):
        return to_docs(outgoing.at[p, inner(g), :], ratio.at[rows(g, src_block), :],
                       cnt_s.at[g, p], cnt_r.at[g, src_block], p)

    def part_copy(g, it, src_block, p):
        return to_docs(part_out.at[it, rows(g, p), :], part_in.at[it, src_block, inner(g), :],
                       part_s.at[g, it, p], part_r.at[g, it, src_block], p)

    def tot_copy(src_block, p):
        return to_docs(tot_out, tot_in.at[src_block], tot_s.at[p], tot_r.at[src_block], p)

    def row_copy(src_block, p):
        return to_tm(row_out, row_in.at[src_block], row_s.at[p], row_r.at[src_block], p)

    groups = range(len(sizes))
    pl.semaphore_wait(barrier, n - 1 + slices - 1)

    def send_first(p):
        load(p).wait()
        outgoing[p, inner(0), :] = raw[p, inner(0), :].astype(F32).astype(BF)
        cnt_copy(0, me, p).start()

    peers(send_first, n, me)

    first = expected_proportions(init_ref[...]).astype(BF)
    for g in groups:
        theta[0, rows(g, me), :] = first[starts[g]:starts[g] + sizes[g]]
    peak = jnp.max(slab_ref[...], axis=0, keepdims=True)
    weights[...] = jnp.exp(slab_ref[...] - peak)
    mass = jnp.sum(weights[...], axis=0, keepdims=True)
    eight = (8, peak.shape[1])
    stat_out[0] = jnp.broadcast_to(peak, eight)
    stat_out[1] = jnp.broadcast_to(mass, eight)
    peers(lambda p: stat_copy(me, p).start(), n, me)
    for g in groups:
        peers(lambda p: theta_copy(g, 0, me, p, me).start(), n, me)

    load(me).wait()
    for g in groups:
        ratio[rows(g, me), :] = raw[me, inner(g), :].astype(F32).astype(BF)
    for g in groups[1:]:
        def send_later(p):
            outgoing[p, inner(g), :] = raw[p, inner(g), :].astype(F32).astype(BF)
            cnt_copy(g - 1, me, p).wait_send()
            cnt_copy(g, me, p).start()

        peers(send_later, n, me)

    stat_in[me] = stat_out[...]
    peers(lambda q: stat_copy(q, q).wait_recv(), n, me)
    all_peaks = [stat_in[q, 0, 0:1, :] for q in range(n)]
    top = functools.reduce(jnp.maximum, all_peaks)
    total_mass = sum(stat_in[q, 1, 0:1, :] * jnp.exp(all_peaks[q] - top) for q in range(n))
    beta[...] = (weights[...] * (jnp.exp(peak - top) / total_mass)).astype(BF)

    prior = prior_ref[...]
    last = ITERS_E - 1
    tiles = words // word_tile

    def tile_columns(i):
        return pl.ds(pl.multiple_of(i * word_tile, word_tile), word_tile)

    def sweep(g, it):
        peers(lambda q: theta_copy(g, it, q, q, q).wait_recv(), n, me)
        if it == 0:
            peers(lambda q: cnt_copy(g, q, q).wait_recv(), n, me)
        own_rows = members(g)
        acc[own_rows, :] = jnp.zeros((sizes[g] * n, acc.shape[1]), F32)

        def sweep_tile(i, carry):
            cols = tile_columns(i)
            tile = beta[cols, :]
            mixture = lax.dot_general(theta[it, own_rows, :], tile, (((1,), (1,)), ((), ())),
                                      preferred_element_type=F32)
            inverse = pl.reciprocal(mixture, approx=True)
            inverse = inverse * (2.0 - mixture * inverse)
            quotient = (ratio[own_rows, cols].astype(F32) * inverse).astype(BF)
            if it == last:
                ratio[own_rows, cols] = quotient
            acc[own_rows, :] += jnp.dot(quotient, tile, preferred_element_type=F32)
            return carry

        lax.fori_loop(0, tiles, sweep_tile, 0)
        part_out[it, own_rows, :] = acc[own_rows, :].astype(BF)
        if not (it == last and g == groups[-1]):
            peers(lambda p: part_copy(g, it, me, p).start(), n, me)

    def settle(g, it):
        part_in[it, me, inner(g), :] = part_out[it, rows(g, me), :]
        peers(lambda q: part_copy(g, it, q, q).wait_recv(), n, me)
        summed = sum(part_in[it, q, inner(g), :].astype(F32) for q in range(n))
        gamma = prior + theta[it, rows(g, me), :].astype(F32) * summed
        if it == last:
            topics_ref[inner(g), :] = gamma
        else:
            theta[it + 1, rows(g, me), :] = expected_proportions(gamma).astype(BF)
            peers(lambda p: theta_copy(g, it + 1, me, p, me).start(), n, me)

    def tally(g, low, high):
        def stats_tile(i, carry):
            cols = tile_columns(i)
            gathered = lax.dot_general(ratio[members(g), cols], theta[last, members(g), :],
                                       (((0,), (0,)), ((), ())), preferred_element_type=F32)
            if g > 0:
                gathered += weights[cols, :]
            if g == groups[-1]:
                gathered = jnp.log(beta[cols, :].astype(F32) * gathered + prior_count)
            weights[cols, :] = gathered
            return carry

        lax.fori_loop(low, high, stats_tile, 0)

    for what, g, it in plan:
        if what == "sweep":
            sweep(g, it)
        elif what == "settle":
            settle(g, it)
        else:
            tally(g, 0, tiles)

    end = groups[-1]
    own = jnp.sum(theta[last].astype(F32) * acc[...], axis=0, keepdims=True)
    tot_out[...] = jnp.broadcast_to(own, eight)
    peers(lambda p: tot_copy(me, p).start(), n, me)
    peers(lambda p: part_copy(end, last, me, p).start(), n, me)
    tally(end, 0, tiles // 2)
    tot_in[me] = tot_out[...]
    peers(lambda q: tot_copy(q, q).wait_recv(), n, me)
    row_out[...] = sum(tot_in[q] for q in range(n))
    peers(lambda p: row_copy(now, p).start(), slices, now)
    tally(end, tiles // 2, tiles)

    row_in[now] = row_out[...]
    peers(lambda q: row_copy(q, q).wait_recv(), slices, now)

    chain = chain_ref[...]
    topics = chain.shape[1]
    previous = initial_scale * chain
    gains, factors = [], []
    for t in range(slices):
        totals = row_in[t, 0:1, :]
        noise = obs_ref[...] * (jnp.sum(totals, axis=1, keepdims=True) / (topics * totals))
        predicted = previous + chain
        gain = predicted / (predicted + noise)
        previous = (1.0 - gain) * predicted
        gains.append(gain)
        factors.append(previous / (previous + chain) if t < slices - 1 else jnp.zeros_like(chain))
    share = [None] * slices
    share[-1] = jnp.ones_like(chain)
    for t in range(slices - 2, -1, -1):
        share[t] = (1.0 - factors[t]) + factors[t] * (1.0 - gains[t + 1]) * share[t + 1]

    def mine(per_slice):
        value = per_slice[0]
        for t in range(1, slices):
            value = jnp.where(now == t, per_slice[t], value)
        return value

    gain, factor, left = mine(gains), mine(factors), mine(share)
    all_words = words * n
    offset = jnp.log((row_in[now, 0:1, :] + prior_count * all_words) / all_words)
    keep = 1.0 - gain
    carried = left * keep
    direct = left * gain

    @pl.when(now == 0)
    def _():
        fwd_in[...] = jnp.zeros_like(fwd_in)

    @pl.when(now == slices - 1)
    def _():
        back_in[...] = jnp.zeros_like(back_in)

    pieces = words // chunk

    def piece(i):
        return pl.ds(pl.multiple_of(i * chunk, chunk), chunk)

    def fwd_copy(i):
        return to_tm(fwd_out.at[piece(i), :], fwd_in.at[piece(i), :], fwd_s.at[i], fwd_r.at[i],
                     lax.rem(now + 1, slices))

    def back_copy(i):
        return to_tm(back_out.at[piece(i), :], back_in.at[piece(i), :], back_s.at[i],
                     back_r.at[i], lax.rem(now + slices - 1, slices))

    lag = slices - 1 - 2 * now
    fwd_lag = jnp.maximum(-lag, 0)
    back_lag = jnp.maximum(lag, 0)
    both_lag = jnp.maximum(fwd_lag, back_lag)

    def step(i, carry):
        f, b, s = i - fwd_lag, i - back_lag, i - both_lag

        @pl.when((f >= 0) & (f < pieces))
        def _():
            @pl.when(now > 0)
            def _():
                fwd_copy(f).wait_recv()

            @pl.when(now < slices - 1)
            def _():
                at = piece(f)
                observed = weights[at, :] - offset
                fwd_out[at, :] = (keep * fwd_in[at, :].astype(F32) + gain * observed).astype(BF)
                fwd_copy(f).start()

        @pl.when((b >= 0) & (b < pieces))
        def _():
            @pl.when(now < slices - 1)
            def _():
                back_copy(b).wait_recv()

            @pl.when(now > 0)
            def _():
                at = piece(b)
                observed = weights[at, :] - offset
                back_out[at, :] = (factor * back_in[at, :].astype(F32)
                                   + direct * observed).astype(BF)
                back_copy(b).start()

        @pl.when((s >= 0) & (s < pieces))
        def _():
            at = piece(s)
            smooth_ref[at, :] = (carried * fwd_in[at, :].astype(F32)
                                 + direct * (weights[at, :] - offset)
                                 + factor * back_in[at, :].astype(F32))
        return carry

    lax.fori_loop(0, pieces + slices - 1, step, 0)
    settle(end, last)

    peers(lambda p: stat_copy(me, p).wait_send(), n, me)
    peers(lambda p: cnt_copy(end, me, p).wait_send(), n, me)
    peers(lambda p: tot_copy(me, p).wait_send(), n, me)
    peers(lambda p: row_copy(now, p).wait_send(), slices, now)
    for it in range(ITERS_E):
        for g in groups:
            peers(lambda p: theta_copy(g, it, me, p, me).wait_send(), n, me)
            peers(lambda p: part_copy(g, it, me, p).wait_send(), n, me)

    def drain(i, carry):
        @pl.when(now < slices - 1)
        def _():
            fwd_copy(i).wait_send()

        @pl.when(now > 0)
        def _():
            back_copy(i).wait_send()
        return carry

    lax.fori_loop(0, pieces, drain, 0)


def body(counts, topic_means, doc_topics_init, dirichlet_prior, chain_var, obs_noise):
    n = lax.axis_size("docs")
    slices = lax.axis_size("tm")
    docs = counts.shape[1]
    words, topics = topic_means.shape[1:]
    every = docs * n
    word_tile = min(512, words // 2)
    chunk = max(words // 16, 16)
    sizes = (docs // 2, docs // 2)
    plan = (("sweep", 0, 0), ("settle", 0, 0), ("sweep", 0, 1), ("settle", 0, 1),
            ("sweep", 1, 0), ("sweep", 0, 2), ("settle", 1, 0), ("settle", 0, 2),
            ("sweep", 1, 1), ("sweep", 0, 3), ("settle", 1, 1), ("tally", 0, 3),
            ("sweep", 1, 2), ("settle", 0, 3), ("settle", 1, 2), ("sweep", 1, 3))
    pieces = words // chunk
    parts = len(sizes)
    dma = pltpu.SemaphoreType.DMA
    vmem = pl.BlockSpec(memory_space=pltpu.VMEM)
    smoothed, doc_topics = pl.pallas_call(
        functools.partial(round_kernel, n, slices, word_tile, chunk, sizes, plan),
        out_shape=(jax.ShapeDtypeStruct((words, topics), F32),
                   jax.ShapeDtypeStruct((docs, topics), F32)),
        in_specs=[pl.BlockSpec(memory_space=pl.ANY)] + [vmem] * 5,
        out_specs=(vmem, vmem),
        scratch_shapes=[
            pltpu.VMEM((n, docs, words), jnp.int32),
            pltpu.VMEM((n, docs, words), BF),
            pltpu.VMEM((every, words), BF),
            pltpu.VMEM((words, topics), F32),
            pltpu.VMEM((words, topics), BF),
            pltpu.VMEM((ITERS_E, every, topics), BF),
            pltpu.VMEM((every, topics), F32),
            pltpu.VMEM((ITERS_E, every, topics), BF),
            pltpu.VMEM((ITERS_E, n, docs, topics), BF),
            pltpu.VMEM((2, 8, topics), F32),
            pltpu.VMEM((n, 2, 8, topics), F32),
            pltpu.VMEM((8, topics), F32),
            pltpu.VMEM((n, 8, topics), F32),
            pltpu.VMEM((8, topics), F32),
            pltpu.VMEM((slices, 8, topics), F32),
            pltpu.VMEM((words, topics), BF),
            pltpu.VMEM((words, topics), BF),
            pltpu.VMEM((words, topics), BF),
            pltpu.VMEM((words, topics), BF),
            dma((n,)),
            dma((parts, n)), dma((parts, n)),
            dma((parts, ITERS_E, n)), dma((parts, ITERS_E, n)),
            dma((parts, ITERS_E, n)), dma((parts, ITERS_E, n)),
            dma((n,)), dma((n,)),
            dma((n,)), dma((n,)),
            dma((slices,)), dma((slices,)),
            dma((pieces,)), dma((pieces,)),
            dma((pieces,)), dma((pieces,)),
        ],
        compiler_params=pltpu.CompilerParams(
            collective_id=0, has_side_effects=True, vmem_limit_bytes=58 * 1024 * 1024),
    )(counts[0], topic_means[0], doc_topics_init[0], dirichlet_prior[None], chain_var[None],
      obs_noise[None])
    return smoothed[None], doc_topics[None]


def solution(mesh):
    in_specs = (P("tm", "docs", None), P("tm", "docs", None), P("tm", "docs", None), P(), P(), P())
    out_specs = (P("tm", "docs", None), P("tm", "docs", None))
    return jax.shard_map(body, mesh=mesh, in_specs=in_specs, out_specs=out_specs, check_vma=False)
```

```python
import functools

import jax
import jax.numpy as jnp
from jax import lax
from jax.experimental import pallas as pl
from jax.experimental.pallas import tpu as pltpu
from jax.sharding import PartitionSpec as P

ITERS_E = 4
prior_count = 0.5
initial_scale = 1000.0
MESH = pl.DeviceIdType.MESH
BF = jnp.bfloat16
F32 = jnp.float32


def expected_proportions(x):
    u = x * (x + 5.0)
    steps = (2.0 * x + 5.0) * (1.0 / u + 1.0 / (u + 4.0) + 1.0 / (u + 6.0))
    y = x + 6.0
    inv = 1.0 / y
    sq = inv * inv
    tail = sq * (1.0 / 12 - sq * (1.0 / 120 - sq * (1.0 / 252 - sq * (1.0 / 240))))
    return jnp.exp(jnp.log(y) - 0.5 * inv - tail - steps)


def round_kernel(n, slices, word_tile, chunk, sizes, plan, counts_ref, slab_ref, init_ref, prior_ref, chain_ref,
                 obs_ref, smooth_ref, topics_ref, raw, outgoing, ratio, weights, beta, theta,
                 acc, part_out, part_in, stat_out, stat_in, tot_out, tot_in, row_out, row_in,
                 fwd_in, back_in, fwd_out, back_out, load_sem, cnt_s, cnt_r, theta_s, theta_r,
                 part_s, part_r, stat_s, stat_r, tot_s, tot_r, row_s, row_r, fwd_s, fwd_r,
                 back_s, back_r):
    docs = init_ref.shape[0]
    words = slab_ref.shape[0]
    me = lax.axis_index("docs")
    now = lax.axis_index("tm")

    def peers(fn, size, own):
        def step(m, carry):
            fn(lax.rem(own + m, size))
            return carry
        lax.fori_loop(1, size, step, 0)

    starts = [sum(sizes[:g]) for g in range(len(sizes))]

    def rows(g, p):
        return pl.ds(pl.multiple_of(starts[g] * n + p * sizes[g], 16), sizes[g])

    def members(g):
        return pl.ds(starts[g] * n, sizes[g] * n)

    def inner(g):
        return pl.ds(starts[g], sizes[g])

    def load(p):
        return pltpu.make_async_copy(
            counts_ref.at[:, pl.ds(pl.multiple_of(p * words, words), words)], raw.at[p],
            load_sem.at[p])

    def to_docs(src, dst, s, r, p):
        return pltpu.make_async_remote_copy(src_ref=src, dst_ref=dst, send_sem=s, recv_sem=r,
                                            device_id={"docs": p}, device_id_type=MESH)

    def to_tm(src, dst, s, r, p):
        return pltpu.make_async_remote_copy(src_ref=src, dst_ref=dst, send_sem=s, recv_sem=r,
                                            device_id={"tm": p}, device_id_type=MESH)

    def load_all(p, carry):
        load(p).start()
        return carry

    lax.fori_loop(0, n, load_all, 0)

    barrier = pltpu.get_barrier_semaphore()
    peers(lambda p: pl.semaphore_signal(barrier, inc=1, device_id={"docs": p},
                                        device_id_type=MESH), n, me)
    peers(lambda p: pl.semaphore_signal(barrier, inc=1, device_id={"tm": p},
                                        device_id_type=MESH), slices, now)

    def theta_copy(g, it, src_block, p, r):
        block = theta.at[it, rows(g, src_block), :]
        return to_docs(block, block, theta_s.at[g, it, p], theta_r.at[g, it, r], p)

    def stat_copy(src_block, p):
        return to_docs(stat_out, stat_in.at[src_block], stat_s.at[p], stat_r.at[src_block], p)

    def cnt_copy(g, src_block, p):
        return to_docs(outgoing.at[p, inner(g), :], ratio.at[rows(g, src_block), :],
                       cnt_s.at[g, p], cnt_r.at[g, src_block], p)

    def part_copy(g, it, src_block, p):
        return to_docs(part_out.at[it, rows(g, p), :], part_in.at[it, src_block, inner(g), :],
                       part_s.at[g, it, p], part_r.at[g, it, src_block], p)

    def tot_copy(src_block, p):
        return to_docs(tot_out, tot_in.at[src_block], tot_s.at[p], tot_r.at[src_block], p)

    def row_copy(src_block, p):
        return to_tm(row_out, row_in.at[src_block], row_s.at[p], row_r.at[src_block], p)

    groups = range(len(sizes))
    pl.semaphore_wait(barrier, n - 1 + slices - 1)

    def send_counts(p):
        load(p).wait()
        outgoing[p] = raw[p].astype(F32).astype(BF)
        for g in groups:
            cnt_copy(g, me, p).start()

    peers(send_counts, n, me)

    first = expected_proportions(init_ref[...]).astype(BF)
    for g in groups:
        theta[0, rows(g, me), :] = first[starts[g]:starts[g] + sizes[g]]
    peak = jnp.max(slab_ref[...], axis=0, keepdims=True)
    weights[...] = jnp.exp(slab_ref[...] - peak)
    mass = jnp.sum(weights[...], axis=0, keepdims=True)
    eight = (8, peak.shape[1])
    stat_out[0] = jnp.broadcast_to(peak, eight)
    stat_out[1] = jnp.broadcast_to(mass, eight)
    peers(lambda p: stat_copy(me, p).start(), n, me)
    for g in groups:
        peers(lambda p: theta_copy(g, 0, me, p, me).start(), n, me)

    load(me).wait()
    for g in groups:
        ratio[rows(g, me), :] = raw[me, inner(g), :].astype(F32).astype(BF)
    stat_in[me] = stat_out[...]
    peers(lambda q: stat_copy(q, q).wait_recv(), n, me)
    all_peaks = [stat_in[q, 0, 0:1, :] for q in range(n)]
    top = functools.reduce(jnp.maximum, all_peaks)
    total_mass = sum(stat_in[q, 1, 0:1, :] * jnp.exp(all_peaks[q] - top) for q in range(n))
    beta[...] = (weights[...] * (jnp.exp(peak - top) / total_mass)).astype(BF)

    prior = prior_ref[...]
    last = ITERS_E - 1
    tiles = words // word_tile

    def tile_columns(i):
        return pl.ds(pl.multiple_of(i * word_tile, word_tile), word_tile)

    def sweep(g, it):
        peers(lambda q: theta_copy(g, it, q, q, q).wait_recv(), n, me)
        if it == 0:
            peers(lambda q: cnt_copy(g, q, q).wait_recv(), n, me)
        own_rows = members(g)
        acc[own_rows, :] = jnp.zeros((sizes[g] * n, acc.shape[1]), F32)

        def sweep_tile(i, carry):
            cols = tile_columns(i)
            tile = beta[cols, :]
            mixture = lax.dot_general(theta[it, own_rows, :], tile, (((1,), (1,)), ((), ())),
                                      preferred_element_type=F32)
            inverse = pl.reciprocal(mixture, approx=True)
            inverse = inverse * (2.0 - mixture * inverse)
            quotient = (ratio[own_rows, cols].astype(F32) * inverse).astype(BF)
            if it == last:
                ratio[own_rows, cols] = quotient
            acc[own_rows, :] += jnp.dot(quotient, tile, preferred_element_type=F32)
            return carry

        lax.fori_loop(0, tiles, sweep_tile, 0)
        part_out[it, own_rows, :] = acc[own_rows, :].astype(BF)
        if not (it == last and g == groups[-1]):
            peers(lambda p: part_copy(g, it, me, p).start(), n, me)

    def settle(g, it):
        part_in[it, me, inner(g), :] = part_out[it, rows(g, me), :]
        peers(lambda q: part_copy(g, it, q, q).wait_recv(), n, me)
        summed = sum(part_in[it, q, inner(g), :].astype(F32) for q in range(n))
        gamma = prior + theta[it, rows(g, me), :].astype(F32) * summed
        if it == last:
            topics_ref[inner(g), :] = gamma
        else:
            theta[it + 1, rows(g, me), :] = expected_proportions(gamma).astype(BF)
            peers(lambda p: theta_copy(g, it + 1, me, p, me).start(), n, me)

    def tally(g, low, high):
        def stats_tile(i, carry):
            cols = tile_columns(i)
            gathered = lax.dot_general(ratio[members(g), cols], theta[last, members(g), :],
                                       (((0,), (0,)), ((), ())), preferred_element_type=F32)
            if g > 0:
                gathered += weights[cols, :]
            if g == groups[-1]:
                gathered = jnp.log(beta[cols, :].astype(F32) * gathered + prior_count)
            weights[cols, :] = gathered
            return carry

        lax.fori_loop(low, high, stats_tile, 0)

    for what, g, it in plan:
        (sweep if what == "sweep" else settle)(g, it)

    end = groups[-1]
    own = jnp.sum(theta[last].astype(F32) * acc[...], axis=0, keepdims=True)
    tot_out[...] = jnp.broadcast_to(own, eight)
    peers(lambda p: tot_copy(me, p).start(), n, me)
    peers(lambda p: part_copy(end, last, me, p).start(), n, me)
    for g in groups[:-1]:
        tally(g, 0, tiles)
    tot_in[me] = tot_out[...]
    peers(lambda q: tot_copy(q, q).wait_recv(), n, me)
    row_out[...] = sum(tot_in[q] for q in range(n))
    peers(lambda p: row_copy(now, p).start(), slices, now)
    tally(end, 0, tiles)

    row_in[now] = row_out[...]
    peers(lambda q: row_copy(q, q).wait_recv(), slices, now)

    chain = chain_ref[...]
    topics = chain.shape[1]
    previous = initial_scale * chain
    gains, factors = [], []
    for t in range(slices):
        totals = row_in[t, 0:1, :]
        noise = obs_ref[...] * (jnp.sum(totals, axis=1, keepdims=True) / (topics * totals))
        predicted = previous + chain
        gain = predicted / (predicted + noise)
        previous = (1.0 - gain) * predicted
        gains.append(gain)
        factors.append(previous / (previous + chain) if t < slices - 1 else jnp.zeros_like(chain))
    share = [None] * slices
    share[-1] = jnp.ones_like(chain)
    for t in range(slices - 2, -1, -1):
        share[t] = (1.0 - factors[t]) + factors[t] * (1.0 - gains[t + 1]) * share[t + 1]

    def mine(per_slice):
        value = per_slice[0]
        for t in range(1, slices):
            value = jnp.where(now == t, per_slice[t], value)
        return value

    gain, factor, left = mine(gains), mine(factors), mine(share)
    all_words = words * n
    offset = jnp.log((row_in[now, 0:1, :] + prior_count * all_words) / all_words)
    keep = 1.0 - gain
    carried = left * keep
    direct = left * gain

    @pl.when(now == 0)
    def _():
        fwd_in[...] = jnp.zeros_like(fwd_in)

    @pl.when(now == slices - 1)
    def _():
        back_in[...] = jnp.zeros_like(back_in)

    pieces = words // chunk

    def piece(i):
        return pl.ds(pl.multiple_of(i * chunk, chunk), chunk)

    def fwd_copy(i):
        return to_tm(fwd_out.at[piece(i), :], fwd_in.at[piece(i), :], fwd_s.at[i], fwd_r.at[i],
                     lax.rem(now + 1, slices))

    def back_copy(i):
        return to_tm(back_out.at[piece(i), :], back_in.at[piece(i), :], back_s.at[i],
                     back_r.at[i], lax.rem(now + slices - 1, slices))

    lag = slices - 1 - 2 * now
    fwd_lag = jnp.maximum(-lag, 0)
    back_lag = jnp.maximum(lag, 0)
    both_lag = jnp.maximum(fwd_lag, back_lag)

    def step(i, carry):
        f, b, s = i - fwd_lag, i - back_lag, i - both_lag

        @pl.when((f >= 0) & (f < pieces))
        def _():
            @pl.when(now > 0)
            def _():
                fwd_copy(f).wait_recv()

            @pl.when(now < slices - 1)
            def _():
                at = piece(f)
                observed = weights[at, :] - offset
                fwd_out[at, :] = (keep * fwd_in[at, :].astype(F32) + gain * observed).astype(BF)
                fwd_copy(f).start()

        @pl.when((b >= 0) & (b < pieces))
        def _():
            @pl.when(now < slices - 1)
            def _():
                back_copy(b).wait_recv()

            @pl.when(now > 0)
            def _():
                at = piece(b)
                observed = weights[at, :] - offset
                back_out[at, :] = (factor * back_in[at, :].astype(F32)
                                   + direct * observed).astype(BF)
                back_copy(b).start()

        @pl.when((s >= 0) & (s < pieces))
        def _():
            at = piece(s)
            smooth_ref[at, :] = (carried * fwd_in[at, :].astype(F32)
                                 + direct * (weights[at, :] - offset)
                                 + factor * back_in[at, :].astype(F32))
        return carry

    lax.fori_loop(0, pieces + slices - 1, step, 0)
    for g in groups:
        settle(g, last)

    peers(lambda p: stat_copy(me, p).wait_send(), n, me)
    for g in groups:
        peers(lambda p: cnt_copy(g, me, p).wait_send(), n, me)
    peers(lambda p: tot_copy(me, p).wait_send(), n, me)
    peers(lambda p: row_copy(now, p).wait_send(), slices, now)
    for it in range(ITERS_E):
        for g in groups:
            peers(lambda p: theta_copy(g, it, me, p, me).wait_send(), n, me)
            peers(lambda p: part_copy(g, it, me, p).wait_send(), n, me)

    def drain(i, carry):
        @pl.when(now < slices - 1)
        def _():
            fwd_copy(i).wait_send()

        @pl.when(now > 0)
        def _():
            back_copy(i).wait_send()
        return carry

    lax.fori_loop(0, pieces, drain, 0)


def body(counts, topic_means, doc_topics_init, dirichlet_prior, chain_var, obs_noise):
    n = lax.axis_size("docs")
    slices = lax.axis_size("tm")
    docs = counts.shape[1]
    words, topics = topic_means.shape[1:]
    every = docs * n
    word_tile = min(512, words // 2)
    chunk = max(words // 16, 16)
    sizes = (docs // 2, docs // 2)
    plan = tuple((what, g, it) for it in range(ITERS_E) for what in ("sweep", "settle")
                 for g in range(len(sizes)) if what == "sweep" or it < ITERS_E - 1)
    pieces = words // chunk
    parts = len(sizes)
    dma = pltpu.SemaphoreType.DMA
    vmem = pl.BlockSpec(memory_space=pltpu.VMEM)
    smoothed, doc_topics = pl.pallas_call(
        functools.partial(round_kernel, n, slices, word_tile, chunk, sizes, plan),
        out_shape=(jax.ShapeDtypeStruct((words, topics), F32),
                   jax.ShapeDtypeStruct((docs, topics), F32)),
        in_specs=[pl.BlockSpec(memory_space=pl.ANY)] + [vmem] * 5,
        out_specs=(vmem, vmem),
        scratch_shapes=[
            pltpu.VMEM((n, docs, words), jnp.int32),
            pltpu.VMEM((n, docs, words), BF),
            pltpu.VMEM((every, words), BF),
            pltpu.VMEM((words, topics), F32),
            pltpu.VMEM((words, topics), BF),
            pltpu.VMEM((ITERS_E, every, topics), BF),
            pltpu.VMEM((every, topics), F32),
            pltpu.VMEM((ITERS_E, every, topics), BF),
            pltpu.VMEM((ITERS_E, n, docs, topics), BF),
            pltpu.VMEM((2, 8, topics), F32),
            pltpu.VMEM((n, 2, 8, topics), F32),
            pltpu.VMEM((8, topics), F32),
            pltpu.VMEM((n, 8, topics), F32),
            pltpu.VMEM((8, topics), F32),
            pltpu.VMEM((slices, 8, topics), F32),
            pltpu.VMEM((words, topics), BF),
            pltpu.VMEM((words, topics), BF),
            pltpu.VMEM((words, topics), BF),
            pltpu.VMEM((words, topics), BF),
            dma((n,)),
            dma((parts, n)), dma((parts, n)),
            dma((parts, ITERS_E, n)), dma((parts, ITERS_E, n)),
            dma((parts, ITERS_E, n)), dma((parts, ITERS_E, n)),
            dma((n,)), dma((n,)),
            dma((n,)), dma((n,)),
            dma((slices,)), dma((slices,)),
            dma((pieces,)), dma((pieces,)),
            dma((pieces,)), dma((pieces,)),
        ],
        compiler_params=pltpu.CompilerParams(
            collective_id=0, has_side_effects=True, vmem_limit_bytes=58 * 1024 * 1024),
    )(counts[0], topic_means[0], doc_topics_init[0], dirichlet_prior[None], chain_var[None],
      obs_noise[None])
    return smoothed[None], doc_topics[None]


def solution(mesh):
    in_specs = (P("tm", "docs", None), P("tm", "docs", None), P("tm", "docs", None), P(), P(), P())
    out_specs = (P("tm", "docs", None), P("tm", "docs", None))
    return jax.shard_map(body, mesh=mesh, in_specs=in_specs, out_specs=out_specs, check_vma=False)
```

```python
import functools

import jax
import jax.numpy as jnp
from jax import lax
from jax.experimental import pallas as pl
from jax.experimental.pallas import tpu as pltpu
from jax.sharding import PartitionSpec as P

ITERS_E = 4
prior_count = 0.5
initial_scale = 1000.0
MESH = pl.DeviceIdType.MESH
BF = jnp.bfloat16
F32 = jnp.float32


def expected_proportions(x):
    u = x * (x + 5.0)
    steps = (2.0 * x + 5.0) * (1.0 / u + 1.0 / (u + 4.0) + 1.0 / (u + 6.0))
    y = x + 6.0
    inv = 1.0 / y
    sq = inv * inv
    tail = sq * (1.0 / 12 - sq * (1.0 / 120 - sq * (1.0 / 252 - sq * (1.0 / 240))))
    return jnp.exp(jnp.log(y) - 0.5 * inv - tail - steps)


def round_kernel(n, slices, word_tile, chunk, sizes, plan, counts_ref, slab_ref, init_ref, prior_ref, chain_ref,
                 obs_ref, smooth_ref, topics_ref, raw, outgoing, ratio, weights, beta, theta,
                 acc, part_out, part_in, stat_out, stat_in, tot_out, tot_in, row_out, row_in,
                 fwd_in, back_in, fwd_out, back_out, load_sem, cnt_s, cnt_r, theta_s, theta_r,
                 part_s, part_r, stat_s, stat_r, tot_s, tot_r, row_s, row_r, fwd_s, fwd_r,
                 back_s, back_r):
    docs = init_ref.shape[0]
    words = slab_ref.shape[0]
    me = lax.axis_index("docs")
    now = lax.axis_index("tm")

    def peers(fn, size, own):
        def step(m, carry):
            fn(lax.rem(own + m, size))
            return carry
        lax.fori_loop(1, size, step, 0)

    starts = [sum(sizes[:g]) for g in range(len(sizes))]

    def rows(g, p):
        return pl.ds(pl.multiple_of(starts[g] * n + p * sizes[g], 16), sizes[g])

    def members(g):
        return pl.ds(starts[g] * n, sizes[g] * n)

    def inner(g):
        return pl.ds(starts[g], sizes[g])

    def load(p):
        return pltpu.make_async_copy(
            counts_ref.at[:, pl.ds(pl.multiple_of(p * words, words), words)], raw.at[p],
            load_sem.at[p])

    def to_docs(src, dst, s, r, p):
        return pltpu.make_async_remote_copy(src_ref=src, dst_ref=dst, send_sem=s, recv_sem=r,
                                            device_id={"docs": p}, device_id_type=MESH)

    def to_tm(src, dst, s, r, p):
        return pltpu.make_async_remote_copy(src_ref=src, dst_ref=dst, send_sem=s, recv_sem=r,
                                            device_id={"tm": p}, device_id_type=MESH)

    def load_all(p, carry):
        load(p).start()
        return carry

    lax.fori_loop(0, n, load_all, 0)

    barrier = pltpu.get_barrier_semaphore()
    peers(lambda p: pl.semaphore_signal(barrier, inc=1, device_id={"docs": p},
                                        device_id_type=MESH), n, me)
    peers(lambda p: pl.semaphore_signal(barrier, inc=1, device_id={"tm": p},
                                        device_id_type=MESH), slices, now)

    def theta_copy(g, it, src_block, p, r):
        block = theta.at[it, rows(g, src_block), :]
        return to_docs(block, block, theta_s.at[g, it, p], theta_r.at[g, it, r], p)

    def stat_copy(src_block, p):
        return to_docs(stat_out, stat_in.at[src_block], stat_s.at[p], stat_r.at[src_block], p)

    def cnt_copy(g, src_block, p):
        return to_docs(outgoing.at[p, inner(g), :], ratio.at[rows(g, src_block), :],
                       cnt_s.at[g, p], cnt_r.at[g, src_block], p)

    def part_copy(g, it, src_block, p):
        return to_docs(part_out.at[it, rows(g, p), :], part_in.at[it, src_block, inner(g), :],
                       part_s.at[g, it, p], part_r.at[g, it, src_block], p)

    def tot_copy(src_block, p):
        return to_docs(tot_out, tot_in.at[src_block], tot_s.at[p], tot_r.at[src_block], p)

    def row_copy(src_block, p):
        return to_tm(row_out, row_in.at[src_block], row_s.at[p], row_r.at[src_block], p)

    groups = range(len(sizes))
    pl.semaphore_wait(barrier, n - 1 + slices - 1)

    def send_counts(p):
        load(p).wait()
        outgoing[p] = raw[p].astype(F32).astype(BF)
        for g in groups:
            cnt_copy(g, me, p).start()

    peers(send_counts, n, me)

    first = expected_proportions(init_ref[...]).astype(BF)
    for g in groups:
        theta[0, rows(g, me), :] = first[starts[g]:starts[g] + sizes[g]]
    peak = jnp.max(slab_ref[...], axis=0, keepdims=True)
    weights[...] = jnp.exp(slab_ref[...] - peak)
    mass = jnp.sum(weights[...], axis=0, keepdims=True)
    eight = (8, peak.shape[1])
    stat_out[0] = jnp.broadcast_to(peak, eight)
    stat_out[1] = jnp.broadcast_to(mass, eight)
    peers(lambda p: stat_copy(me, p).start(), n, me)
    for g in groups:
        peers(lambda p: theta_copy(g, 0, me, p, me).start(), n, me)

    load(me).wait()
    for g in groups:
        ratio[rows(g, me), :] = raw[me, inner(g), :].astype(F32).astype(BF)
    stat_in[me] = stat_out[...]
    peers(lambda q: stat_copy(q, q).wait_recv(), n, me)
    all_peaks = [stat_in[q, 0, 0:1, :] for q in range(n)]
    top = functools.reduce(jnp.maximum, all_peaks)
    total_mass = sum(stat_in[q, 1, 0:1, :] * jnp.exp(all_peaks[q] - top) for q in range(n))
    beta[...] = (weights[...] * (jnp.exp(peak - top) / total_mass)).astype(BF)

    prior = prior_ref[...]
    last = ITERS_E - 1
    tiles = words // word_tile

    def tile_columns(i):
        return pl.ds(pl.multiple_of(i * word_tile, word_tile), word_tile)

    def sweep(g, it):
        peers(lambda q: theta_copy(g, it, q, q, q).wait_recv(), n, me)
        if it == 0:
            peers(lambda q: cnt_copy(g, q, q).wait_recv(), n, me)
        own_rows = members(g)
        acc[own_rows, :] = jnp.zeros((sizes[g] * n, acc.shape[1]), F32)

        def sweep_tile(i, carry):
            cols = tile_columns(i)
            tile = beta[cols, :]
            mixture = lax.dot_general(theta[it, own_rows, :], tile, (((1,), (1,)), ((), ())),
                                      preferred_element_type=F32)
            inverse = pl.reciprocal(mixture, approx=True)
            inverse = inverse * (2.0 - mixture * inverse)
            quotient = (ratio[own_rows, cols].astype(F32) * inverse).astype(BF)
            if it == last:
                ratio[own_rows, cols] = quotient
            acc[own_rows, :] += jnp.dot(quotient, tile, preferred_element_type=F32)
            return carry

        lax.fori_loop(0, tiles, sweep_tile, 0, unroll=2)
        part_out[it, own_rows, :] = acc[own_rows, :].astype(BF)
        if not (it == last and g == groups[-1]):
            peers(lambda p: part_copy(g, it, me, p).start(), n, me)

    def settle(g, it):
        part_in[it, me, inner(g), :] = part_out[it, rows(g, me), :]
        peers(lambda q: part_copy(g, it, q, q).wait_recv(), n, me)
        summed = sum(part_in[it, q, inner(g), :].astype(F32) for q in range(n))
        gamma = prior + theta[it, rows(g, me), :].astype(F32) * summed
        if it == last:
            topics_ref[inner(g), :] = gamma
        else:
            theta[it + 1, rows(g, me), :] = expected_proportions(gamma).astype(BF)
            peers(lambda p: theta_copy(g, it + 1, me, p, me).start(), n, me)

    def tally(g, low, high):
        def stats_tile(i, carry):
            cols = tile_columns(i)
            gathered = lax.dot_general(ratio[members(g), cols], theta[last, members(g), :],
                                       (((0,), (0,)), ((), ())), preferred_element_type=F32)
            if g > 0:
                gathered += weights[cols, :]
            if g == groups[-1]:
                gathered = jnp.log(beta[cols, :].astype(F32) * gathered + prior_count)
            weights[cols, :] = gathered
            return carry

        lax.fori_loop(low, high, stats_tile, 0)

    for what, g, it in plan:
        (sweep if what == "sweep" else settle)(g, it)

    end = groups[-1]
    own = jnp.sum(theta[last].astype(F32) * acc[...], axis=0, keepdims=True)
    tot_out[...] = jnp.broadcast_to(own, eight)
    peers(lambda p: tot_copy(me, p).start(), n, me)
    peers(lambda p: part_copy(end, last, me, p).start(), n, me)
    for g in groups[:-1]:
        tally(g, 0, tiles)
    tot_in[me] = tot_out[...]
    peers(lambda q: tot_copy(q, q).wait_recv(), n, me)
    row_out[...] = sum(tot_in[q] for q in range(n))
    peers(lambda p: row_copy(now, p).start(), slices, now)
    tally(end, 0, tiles)

    row_in[now] = row_out[...]
    peers(lambda q: row_copy(q, q).wait_recv(), slices, now)

    chain = chain_ref[...]
    topics = chain.shape[1]
    previous = initial_scale * chain
    gains, factors = [], []
    for t in range(slices):
        totals = row_in[t, 0:1, :]
        noise = obs_ref[...] * (jnp.sum(totals, axis=1, keepdims=True) / (topics * totals))
        predicted = previous + chain
        gain = predicted / (predicted + noise)
        previous = (1.0 - gain) * predicted
        gains.append(gain)
        factors.append(previous / (previous + chain) if t < slices - 1 else jnp.zeros_like(chain))
    share = [None] * slices
    share[-1] = jnp.ones_like(chain)
    for t in range(slices - 2, -1, -1):
        share[t] = (1.0 - factors[t]) + factors[t] * (1.0 - gains[t + 1]) * share[t + 1]

    def mine(per_slice):
        value = per_slice[0]
        for t in range(1, slices):
            value = jnp.where(now == t, per_slice[t], value)
        return value

    gain, factor, left = mine(gains), mine(factors), mine(share)
    all_words = words * n
    offset = jnp.log((row_in[now, 0:1, :] + prior_count * all_words) / all_words)
    keep = 1.0 - gain
    carried = left * keep
    direct = left * gain

    @pl.when(now == 0)
    def _():
        fwd_in[...] = jnp.zeros_like(fwd_in)

    @pl.when(now == slices - 1)
    def _():
        back_in[...] = jnp.zeros_like(back_in)

    pieces = words // chunk

    def piece(i):
        return pl.ds(pl.multiple_of(i * chunk, chunk), chunk)

    def fwd_copy(i):
        return to_tm(fwd_out.at[piece(i), :], fwd_in.at[piece(i), :], fwd_s.at[i], fwd_r.at[i],
                     lax.rem(now + 1, slices))

    def back_copy(i):
        return to_tm(back_out.at[piece(i), :], back_in.at[piece(i), :], back_s.at[i],
                     back_r.at[i], lax.rem(now + slices - 1, slices))

    lag = slices - 1 - 2 * now
    fwd_lag = jnp.maximum(-lag, 0)
    back_lag = jnp.maximum(lag, 0)
    both_lag = jnp.maximum(fwd_lag, back_lag)

    def step(i, carry):
        f, b, s = i - fwd_lag, i - back_lag, i - both_lag

        @pl.when((f >= 0) & (f < pieces))
        def _():
            @pl.when(now > 0)
            def _():
                fwd_copy(f).wait_recv()

            @pl.when(now < slices - 1)
            def _():
                at = piece(f)
                observed = weights[at, :] - offset
                fwd_out[at, :] = (keep * fwd_in[at, :].astype(F32) + gain * observed).astype(BF)
                fwd_copy(f).start()

        @pl.when((b >= 0) & (b < pieces))
        def _():
            @pl.when(now < slices - 1)
            def _():
                back_copy(b).wait_recv()

            @pl.when(now > 0)
            def _():
                at = piece(b)
                observed = weights[at, :] - offset
                back_out[at, :] = (factor * back_in[at, :].astype(F32)
                                   + direct * observed).astype(BF)
                back_copy(b).start()

        @pl.when((s >= 0) & (s < pieces))
        def _():
            at = piece(s)
            smooth_ref[at, :] = (carried * fwd_in[at, :].astype(F32)
                                 + direct * (weights[at, :] - offset)
                                 + factor * back_in[at, :].astype(F32))
        return carry

    lax.fori_loop(0, pieces + slices - 1, step, 0)
    for g in groups:
        settle(g, last)

    peers(lambda p: stat_copy(me, p).wait_send(), n, me)
    for g in groups:
        peers(lambda p: cnt_copy(g, me, p).wait_send(), n, me)
    peers(lambda p: tot_copy(me, p).wait_send(), n, me)
    peers(lambda p: row_copy(now, p).wait_send(), slices, now)
    for it in range(ITERS_E):
        for g in groups:
            peers(lambda p: theta_copy(g, it, me, p, me).wait_send(), n, me)
            peers(lambda p: part_copy(g, it, me, p).wait_send(), n, me)

    def drain(i, carry):
        @pl.when(now < slices - 1)
        def _():
            fwd_copy(i).wait_send()

        @pl.when(now > 0)
        def _():
            back_copy(i).wait_send()
        return carry

    lax.fori_loop(0, pieces, drain, 0)


def body(counts, topic_means, doc_topics_init, dirichlet_prior, chain_var, obs_noise):
    n = lax.axis_size("docs")
    slices = lax.axis_size("tm")
    docs = counts.shape[1]
    words, topics = topic_means.shape[1:]
    every = docs * n
    word_tile = min(512, words // 2)
    chunk = max(words // 8, 16)
    sizes = (docs,)
    plan = tuple((what, g, it) for it in range(ITERS_E) for what in ("sweep", "settle")
                 for g in range(len(sizes)) if what == "sweep" or it < ITERS_E - 1)
    pieces = words // chunk
    parts = len(sizes)
    dma = pltpu.SemaphoreType.DMA
    vmem = pl.BlockSpec(memory_space=pltpu.VMEM)
    smoothed, doc_topics = pl.pallas_call(
        functools.partial(round_kernel, n, slices, word_tile, chunk, sizes, plan),
        out_shape=(jax.ShapeDtypeStruct((words, topics), F32),
                   jax.ShapeDtypeStruct((docs, topics), F32)),
        in_specs=[pl.BlockSpec(memory_space=pl.ANY)] + [vmem] * 5,
        out_specs=(vmem, vmem),
        scratch_shapes=[
            pltpu.VMEM((n, docs, words), jnp.int32),
            pltpu.VMEM((n, docs, words), BF),
            pltpu.VMEM((every, words), BF),
            pltpu.VMEM((words, topics), F32),
            pltpu.VMEM((words, topics), BF),
            pltpu.VMEM((ITERS_E, every, topics), BF),
            pltpu.VMEM((every, topics), F32),
            pltpu.VMEM((ITERS_E, every, topics), BF),
            pltpu.VMEM((ITERS_E, n, docs, topics), BF),
            pltpu.VMEM((2, 8, topics), F32),
            pltpu.VMEM((n, 2, 8, topics), F32),
            pltpu.VMEM((8, topics), F32),
            pltpu.VMEM((n, 8, topics), F32),
            pltpu.VMEM((8, topics), F32),
            pltpu.VMEM((slices, 8, topics), F32),
            pltpu.VMEM((words, topics), BF),
            pltpu.VMEM((words, topics), BF),
            pltpu.VMEM((words, topics), BF),
            pltpu.VMEM((words, topics), BF),
            dma((n,)),
            dma((parts, n)), dma((parts, n)),
            dma((parts, ITERS_E, n)), dma((parts, ITERS_E, n)),
            dma((parts, ITERS_E, n)), dma((parts, ITERS_E, n)),
            dma((n,)), dma((n,)),
            dma((n,)), dma((n,)),
            dma((slices,)), dma((slices,)),
            dma((pieces,)), dma((pieces,)),
            dma((pieces,)), dma((pieces,)),
        ],
        compiler_params=pltpu.CompilerParams(
            collective_id=0, has_side_effects=True, vmem_limit_bytes=58 * 1024 * 1024),
    )(counts[0], topic_means[0], doc_topics_init[0], dirichlet_prior[None], chain_var[None],
      obs_noise[None])
    return smoothed[None], doc_topics[None]


def solution(mesh):
    in_specs = (P("tm", "docs", None), P("tm", "docs", None), P("tm", "docs", None), P(), P(), P())
    out_specs = (P("tm", "docs", None), P("tm", "docs", None))
    return jax.shard_map(body, mesh=mesh, in_specs=in_specs, out_specs=out_specs, check_vma=False)
```

```python
import functools

import jax
import jax.numpy as jnp
from jax import lax
from jax.experimental import pallas as pl
from jax.experimental.pallas import tpu as pltpu
from jax.sharding import PartitionSpec as P

ITERS_E = 4
prior_count = 0.5
initial_scale = 1000.0
MESH = pl.DeviceIdType.MESH
BF = jnp.bfloat16
F32 = jnp.float32


def expected_proportions(x):
    u = x * (x + 5.0)
    steps = (2.0 * x + 5.0) * (1.0 / u + 1.0 / (u + 4.0) + 1.0 / (u + 6.0))
    y = x + 6.0
    inv = 1.0 / y
    sq = inv * inv
    tail = sq * (1.0 / 12 - sq * (1.0 / 120 - sq * (1.0 / 252 - sq * (1.0 / 240))))
    return jnp.exp(jnp.log(y) - 0.5 * inv - tail - steps)


def round_kernel(n, slices, word_tile, chunk, counts_ref, slab_ref, init_ref, prior_ref, chain_ref,
                 obs_ref, smooth_ref, topics_ref, raw, outgoing, ratio, weights, beta, theta,
                 acc, part_out, part_in, stat_out, stat_in, tot_out, tot_in, row_out, row_in,
                 fwd_in, back_in, fwd_out, back_out, load_sem, cnt_s, cnt_r, theta_s, theta_r,
                 part_s, part_r, stat_s, stat_r, tot_s, tot_r, row_s, row_r, fwd_s, fwd_r,
                 back_s, back_r):
    docs = init_ref.shape[0]
    words = slab_ref.shape[0]
    me = lax.axis_index("docs")
    now = lax.axis_index("tm")

    def peers(fn, size, own):
        for m in range(1, size):
            fn(m, lax.rem(own + m, size))

    def wait_bytes(ref, sem):
        pltpu.make_async_copy(ref, ref, sem).wait()

    def rows(p):
        return pl.ds(pl.multiple_of(p * docs, docs), docs)

    others = pl.ds(0, (n - 1) * docs)

    def load(p):
        return pltpu.make_async_copy(
            counts_ref.at[:, pl.ds(pl.multiple_of(p * words, words), words)], raw.at[p],
            load_sem.at[p])

    def to_docs(src, dst, s, r, p):
        return pltpu.make_async_remote_copy(src_ref=src, dst_ref=dst, send_sem=s, recv_sem=r,
                                            device_id={"docs": p}, device_id_type=MESH)

    def to_tm(src, dst, s, r, p):
        return pltpu.make_async_remote_copy(src_ref=src, dst_ref=dst, send_sem=s, recv_sem=r,
                                            device_id={"tm": p}, device_id_type=MESH)

    def load_all(p, carry):
        load(p).start()
        return carry

    lax.fori_loop(0, n, load_all, 0)

    barrier = pltpu.get_barrier_semaphore()
    peers(lambda m, p: pl.semaphore_signal(barrier, inc=1, device_id={"docs": p},
                                           device_id_type=MESH), n, me)
    peers(lambda m, p: pl.semaphore_signal(barrier, inc=1, device_id={"tm": p},
                                           device_id_type=MESH), slices, now)

    def send_theta(it):
        block = theta.at[it, rows(me), :]
        peers(lambda m, p: to_docs(block, block, theta_s.at[it], theta_r.at[it], p).start(), n, me)

    def send_parts(it):
        peers(lambda m, p: to_docs(part_out.at[it, rows(p), :], part_in.at[it, m - 1],
                                   part_s.at[it], part_r.at[it], p).start(), n, me)

    pl.semaphore_wait(barrier, n - 1 + slices - 1)

    def send_counts(m, carry):
        p = lax.rem(me + m, n)
        load(p).wait()
        outgoing[m - 1] = raw[p].astype(F32).astype(BF)
        to_docs(outgoing.at[m - 1], ratio.at[rows(me), :], cnt_s.at[0], cnt_r.at[0], p).start()
        return carry

    lax.fori_loop(1, n, send_counts, 0)

    theta[0, rows(me), :] = expected_proportions(init_ref[...]).astype(BF)
    peak = jnp.max(slab_ref[...], axis=0, keepdims=True)
    weights[...] = jnp.exp(slab_ref[...] - peak)
    mass = jnp.sum(weights[...], axis=0, keepdims=True)
    eight = (8, peak.shape[1])
    stat_out[0] = jnp.broadcast_to(peak, eight)
    stat_out[1] = jnp.broadcast_to(mass, eight)
    peers(lambda m, p: to_docs(stat_out, stat_in.at[m - 1], stat_s.at[0], stat_r.at[0], p).start(),
          n, me)
    send_theta(0)

    load(me).wait()
    ratio[rows(me), :] = raw[me].astype(F32).astype(BF)

    stat_in[n - 1] = stat_out[...]
    wait_bytes(stat_in.at[pl.ds(0, n - 1)], stat_r.at[0])
    all_peaks = [stat_in[q, 0, 0:1, :] for q in range(n)]
    top = functools.reduce(jnp.maximum, all_peaks)
    total_mass = sum(stat_in[q, 1, 0:1, :] * jnp.exp(all_peaks[q] - top) for q in range(n))
    beta[...] = (weights[...] * (jnp.exp(peak - top) / total_mass)).astype(BF)

    prior = prior_ref[...]
    last = ITERS_E - 1
    tiles = words // word_tile

    def tile_columns(i):
        return pl.ds(pl.multiple_of(i * word_tile, word_tile), word_tile)

    def sweep(it):
        wait_bytes(theta.at[it, others, :], theta_r.at[it])
        if it == 0:
            wait_bytes(ratio.at[others, :], cnt_r.at[0])
        acc[...] = jnp.zeros_like(acc)

        def sweep_tile(i, carry):
            cols = tile_columns(i)
            tile = beta[cols, :]
            mixture = lax.dot_general(theta[it], tile, (((1,), (1,)), ((), ())),
                                      preferred_element_type=F32)
            inverse = pl.reciprocal(mixture, approx=True)
            inverse = inverse * (2.0 - mixture * inverse)
            quotient = (ratio[:, cols].astype(F32) * inverse).astype(BF)
            if it == last:
                ratio[:, cols] = quotient
            acc[...] += jnp.dot(quotient, tile, preferred_element_type=F32)
            return carry

        lax.fori_loop(0, tiles, sweep_tile, 0, unroll=2)
        part_out[it] = acc[...].astype(BF)

    def settle(it):
        part_in[it, n - 1] = part_out[it, rows(me), :]
        wait_bytes(part_in.at[it, pl.ds(0, n - 1)], part_r.at[it])
        summed = sum(part_in[it, q].astype(F32) for q in range(n))
        return prior + theta[it, rows(me), :].astype(F32) * summed

    def stats_tile(i, carry):
        cols = tile_columns(i)
        gathered = lax.dot_general(ratio[:, cols], theta[last], (((0,), (0,)), ((), ())),
                                   preferred_element_type=F32)
        weights[cols, :] = jnp.log(beta[cols, :].astype(F32) * gathered + prior_count)
        return carry

    for it in range(last):
        sweep(it)
        send_parts(it)
        theta[it + 1, rows(me), :] = expected_proportions(settle(it)).astype(BF)
        send_theta(it + 1)

    sweep(last)
    own = jnp.sum(theta[last].astype(F32) * acc[...], axis=0, keepdims=True)
    tot_out[...] = jnp.broadcast_to(own, eight)
    peers(lambda m, p: to_docs(tot_out, tot_in.at[m - 1], tot_s.at[0], tot_r.at[0], p).start(),
          n, me)
    send_parts(last)
    lax.fori_loop(0, tiles // 2, stats_tile, 0)
    tot_in[n - 1] = tot_out[...]
    wait_bytes(tot_in.at[pl.ds(0, n - 1)], tot_r.at[0])
    row_out[...] = sum(tot_in[q] for q in range(n))
    peers(lambda m, p: to_tm(row_out, row_in.at[now], row_s.at[0], row_r.at[0], p).start(),
          slices, now)
    lax.fori_loop(tiles // 2, tiles, stats_tile, 0)

    row_in[now] = row_out[...]
    wait_bytes(row_in.at[pl.ds(0, slices - 1)], row_r.at[0])

    chain = chain_ref[...]
    topics = chain.shape[1]
    previous = initial_scale * chain
    gains, factors = [], []
    for t in range(slices):
        totals = row_in[t, 0:1, :]
        noise = obs_ref[...] * (jnp.sum(totals, axis=1, keepdims=True) / (topics * totals))
        predicted = previous + chain
        gain = predicted / (predicted + noise)
        previous = (1.0 - gain) * predicted
        gains.append(gain)
        factors.append(previous / (previous + chain) if t < slices - 1 else jnp.zeros_like(chain))
    share = [None] * slices
    share[-1] = jnp.ones_like(chain)
    for t in range(slices - 2, -1, -1):
        share[t] = (1.0 - factors[t]) + factors[t] * (1.0 - gains[t + 1]) * share[t + 1]

    def mine(per_slice):
        value = per_slice[0]
        for t in range(1, slices):
            value = jnp.where(now == t, per_slice[t], value)
        return value

    gain, factor, left = mine(gains), mine(factors), mine(share)
    all_words = words * n
    offset = jnp.log((row_in[now, 0:1, :] + prior_count * all_words) / all_words)
    keep = 1.0 - gain
    carried = left * keep
    direct = left * gain

    @pl.when(now == 0)
    def _():
        fwd_in[...] = jnp.zeros_like(fwd_in)

    @pl.when(now == slices - 1)
    def _():
        back_in[...] = jnp.zeros_like(back_in)

    pieces = words // chunk

    def piece(i):
        return pl.ds(pl.multiple_of(i * chunk, chunk), chunk)

    def fwd_copy(i):
        return to_tm(fwd_out.at[piece(i), :], fwd_in.at[piece(i), :], fwd_s.at[i], fwd_r.at[i],
                     lax.rem(now + 1, slices))

    def back_copy(i):
        return to_tm(back_out.at[piece(i), :], back_in.at[piece(i), :], back_s.at[i],
                     back_r.at[i], lax.rem(now + slices - 1, slices))

    lag = 2 * (slices - 1 - 2 * now)
    fwd_lag = jnp.maximum(-lag, 0)
    back_lag = jnp.maximum(lag, 0)
    both_lag = jnp.maximum(fwd_lag, back_lag)

    def step(i, carry):
        f, b, s = i - fwd_lag, i - back_lag, i - both_lag

        @pl.when((f >= 0) & (f < pieces))
        def _():
            @pl.when(now > 0)
            def _():
                fwd_copy(f).wait_recv()

            @pl.when(now < slices - 1)
            def _():
                at = piece(f)
                observed = weights[at, :] - offset
                fwd_out[at, :] = (keep * fwd_in[at, :].astype(F32) + gain * observed).astype(BF)
                fwd_copy(f).start()

        @pl.when((b >= 0) & (b < pieces))
        def _():
            @pl.when(now < slices - 1)
            def _():
                back_copy(b).wait_recv()

            @pl.when(now > 0)
            def _():
                at = piece(b)
                observed = weights[at, :] - offset
                back_out[at, :] = (factor * back_in[at, :].astype(F32)
                                   + direct * observed).astype(BF)
                back_copy(b).start()

        @pl.when((s >= 0) & (s < pieces))
        def _():
            at = piece(s)
            smoothed = (carried * fwd_in[at, :].astype(F32)
                        + direct * (weights[at, :] - offset)
                        + factor * back_in[at, :].astype(F32))
            smooth_ref[at, :] = smoothed.astype(BF)
        return carry

    lax.fori_loop(0, pieces + 2 * (slices - 1), step, 0)
    topics_ref[...] = settle(last)

    wait_bytes(stat_in.at[pl.ds(0, n - 1)], stat_s.at[0])
    wait_bytes(ratio.at[others, :], cnt_s.at[0])
    wait_bytes(tot_in.at[pl.ds(0, n - 1)], tot_s.at[0])
    wait_bytes(row_in.at[pl.ds(0, slices - 1)], row_s.at[0])
    for it in range(ITERS_E):
        wait_bytes(theta.at[it, others, :], theta_s.at[it])
        wait_bytes(part_in.at[it, pl.ds(0, n - 1)], part_s.at[it])

    def drain(i, carry):
        @pl.when(now < slices - 1)
        def _():
            fwd_copy(i).wait_send()

        @pl.when(now > 0)
        def _():
            back_copy(i).wait_send()
        return carry

    lax.fori_loop(0, pieces, drain, 0)


def body(counts, topic_means, doc_topics_init, dirichlet_prior, chain_var, obs_noise):
    n = lax.axis_size("docs")
    slices = lax.axis_size("tm")
    docs = counts.shape[1]
    words, topics = topic_means.shape[1:]
    every = docs * n
    word_tile = min(512, words // 2)
    chunk = max(words // 16, 16)
    pieces = words // chunk
    dma = pltpu.SemaphoreType.DMA
    vmem = pl.BlockSpec(memory_space=pltpu.VMEM)
    smoothed, doc_topics = pl.pallas_call(
        functools.partial(round_kernel, n, slices, word_tile, chunk),
        out_shape=(jax.ShapeDtypeStruct((words, topics), BF),
                   jax.ShapeDtypeStruct((docs, topics), F32)),
        in_specs=[pl.BlockSpec(memory_space=pl.ANY)] + [vmem] * 5,
        out_specs=(vmem, vmem),
        scratch_shapes=[
            pltpu.VMEM((n, docs, words), jnp.int32),
            pltpu.VMEM((n - 1, docs, words), BF),
            pltpu.VMEM((every, words), BF),
            pltpu.VMEM((words, topics), F32),
            pltpu.VMEM((words, topics), BF),
            pltpu.VMEM((ITERS_E, every, topics), BF),
            pltpu.VMEM((every, topics), F32),
            pltpu.VMEM((ITERS_E, every, topics), BF),
            pltpu.VMEM((ITERS_E, n, docs, topics), BF),
            pltpu.VMEM((2, 8, topics), F32),
            pltpu.VMEM((n, 2, 8, topics), F32),
            pltpu.VMEM((8, topics), F32),
            pltpu.VMEM((n, 8, topics), F32),
            pltpu.VMEM((8, topics), F32),
            pltpu.VMEM((slices, 8, topics), F32),
            pltpu.VMEM((words, topics), BF),
            pltpu.VMEM((words, topics), BF),
            pltpu.VMEM((words, topics), BF),
            pltpu.VMEM((words, topics), BF),
            dma((n,)),
            dma((1,)), dma((1,)),
            dma((ITERS_E,)), dma((ITERS_E,)),
            dma((ITERS_E,)), dma((ITERS_E,)),
            dma((1,)), dma((1,)),
            dma((1,)), dma((1,)),
            dma((1,)), dma((1,)),
            dma((pieces,)), dma((pieces,)),
            dma((pieces,)), dma((pieces,)),
        ],
        compiler_params=pltpu.CompilerParams(
            collective_id=0, has_side_effects=True, vmem_limit_bytes=58 * 1024 * 1024),
    )(counts[0], topic_means[0], doc_topics_init[0], dirichlet_prior[None], chain_var[None],
      obs_noise[None])
    return smoothed.astype(F32)[None], doc_topics[None]


def solution(mesh):
    in_specs = (P("tm", "docs", None), P("tm", "docs", None), P("tm", "docs", None), P(), P(), P())
    out_specs = (P("tm", "docs", None), P("tm", "docs", None))
    return jax.shard_map(body, mesh=mesh, in_specs=in_specs, out_specs=out_specs, check_vma=False)
```

```python
import functools

import jax
import jax.numpy as jnp
from jax import lax
from jax.experimental import pallas as pl
from jax.experimental.pallas import tpu as pltpu
from jax.sharding import PartitionSpec as P

ITERS_E = 4
prior_count = 0.5
initial_scale = 1000.0
MESH = pl.DeviceIdType.MESH
BF = jnp.bfloat16
F32 = jnp.float32


def expected_proportions(x):
    u = x * (x + 5.0)
    steps = (2.0 * x + 5.0) * (1.0 / u + 1.0 / (u + 4.0) + 1.0 / (u + 6.0))
    y = x + 6.0
    inv = 1.0 / y
    sq = inv * inv
    tail = sq * (1.0 / 12 - sq * (1.0 / 120 - sq * (1.0 / 252 - sq * (1.0 / 240))))
    return jnp.exp(jnp.log(y) - 0.5 * inv - tail - steps)


def round_kernel(n, slices, word_tile, chunk, rounds, counts_ref, slab_ref, init_ref, prior_ref, chain_ref,
                 obs_ref, smooth_ref, topics_ref, raw, outgoing, ratio, weights, beta, theta,
                 acc, part_out, part_in, stat_out, stat_in, tot_out, tot_in, row_out, row_in,
                 fwd_in, back_in, fwd_out, back_out, load_sem, cnt_s, cnt_r, theta_s, theta_r,
                 part_s, part_r, stat_s, stat_r, tot_s, tot_r, row_s, row_r, fwd_s, fwd_r,
                 back_s, back_r):
    docs = init_ref.shape[0]
    words = slab_ref.shape[0]
    me = lax.axis_index("docs")
    now = lax.axis_index("tm")

    def peers(fn, size, own):
        for m in range(1, size):
            fn(m, lax.rem(own + m, size))

    def wait_bytes(ref, sem):
        pltpu.make_async_copy(ref, ref, sem).wait()

    def rows(p):
        return pl.ds(pl.multiple_of(p * docs, docs), docs)

    others = pl.ds(0, (n - 1) * docs)

    def load(p):
        return pltpu.make_async_copy(
            counts_ref.at[:, pl.ds(pl.multiple_of(p * words, words), words)], raw.at[p],
            load_sem.at[p])

    def to_docs(src, dst, s, r, p):
        return pltpu.make_async_remote_copy(src_ref=src, dst_ref=dst, send_sem=s, recv_sem=r,
                                            device_id={"docs": p}, device_id_type=MESH)

    def to_tm(src, dst, s, r, p):
        return pltpu.make_async_remote_copy(src_ref=src, dst_ref=dst, send_sem=s, recv_sem=r,
                                            device_id={"tm": p}, device_id_type=MESH)

    def load_all(p, carry):
        load(p).start()
        return carry

    lax.fori_loop(0, n, load_all, 0)

    barrier = pltpu.get_barrier_semaphore()
    peers(lambda m, p: pl.semaphore_signal(barrier, inc=1, device_id={"docs": p},
                                           device_id_type=MESH), n, me)
    peers(lambda m, p: pl.semaphore_signal(barrier, inc=1, device_id={"tm": p},
                                           device_id_type=MESH), slices, now)

    def send_theta(it):
        block = theta.at[it, rows(me), :]
        peers(lambda m, p: to_docs(block, block, theta_s.at[it], theta_r.at[it], p).start(), n, me)

    def send_parts(it):
        peers(lambda m, p: to_docs(part_out.at[it, rows(p), :], part_in.at[it, m - 1],
                                   part_s.at[it], part_r.at[it], p).start(), n, me)

    pl.semaphore_wait(barrier, n - 1 + slices - 1)

    part = docs // rounds

    def send_part(m, r):
        span = pl.ds(pl.multiple_of(r * part, part), part)
        there = pl.ds(pl.multiple_of(me * docs + r * part, part), part)
        to_docs(outgoing.at[m - 1, span, :], ratio.at[there, :], cnt_s.at[0], cnt_r.at[0],
                lax.rem(me + m, n)).start()

    def first_round(m, carry):
        p = lax.rem(me + m, n)
        load(p).wait()
        outgoing[m - 1] = raw[p].astype(F32).astype(BF)
        send_part(m, 0)
        return carry

    lax.fori_loop(1, n, first_round, 0)

    theta[0, rows(me), :] = expected_proportions(init_ref[...]).astype(BF)
    peak = jnp.max(slab_ref[...], axis=0, keepdims=True)
    weights[...] = jnp.exp(slab_ref[...] - peak)
    mass = jnp.sum(weights[...], axis=0, keepdims=True)
    eight = (8, peak.shape[1])
    stat_out[0] = jnp.broadcast_to(peak, eight)
    stat_out[1] = jnp.broadcast_to(mass, eight)
    peers(lambda m, p: to_docs(stat_out, stat_in.at[m - 1], stat_s.at[0], stat_r.at[0], p).start(),
          n, me)
    send_theta(0)

    def later_rounds(i, carry):
        send_part(1 + lax.rem(i, n - 1), 1 + i // (n - 1))
        return carry

    lax.fori_loop(0, (rounds - 1) * (n - 1), later_rounds, 0)
    load(me).wait()
    ratio[rows(me), :] = raw[me].astype(F32).astype(BF)

    stat_in[n - 1] = stat_out[...]
    wait_bytes(stat_in.at[pl.ds(0, n - 1)], stat_r.at[0])
    all_peaks = [stat_in[q, 0, 0:1, :] for q in range(n)]
    top = functools.reduce(jnp.maximum, all_peaks)
    total_mass = sum(stat_in[q, 1, 0:1, :] * jnp.exp(all_peaks[q] - top) for q in range(n))
    beta[...] = (weights[...] * (jnp.exp(peak - top) / total_mass)).astype(BF)

    prior = prior_ref[...]
    last = ITERS_E - 1
    tiles = words // word_tile

    def tile_columns(i):
        return pl.ds(pl.multiple_of(i * word_tile, word_tile), word_tile)

    def sweep(it):
        wait_bytes(theta.at[it, others, :], theta_r.at[it])
        if it == 0:
            wait_bytes(ratio.at[others, :], cnt_r.at[0])
        acc[...] = jnp.zeros_like(acc)

        def sweep_tile(i, carry):
            cols = tile_columns(i)
            tile = beta[cols, :]
            mixture = lax.dot_general(theta[it], tile, (((1,), (1,)), ((), ())),
                                      preferred_element_type=F32)
            inverse = pl.reciprocal(mixture, approx=True)
            inverse = inverse * (2.0 - mixture * inverse)
            quotient = ratio[:, cols] * inverse.astype(BF)
            if it == last:
                ratio[:, cols] = quotient
            acc[...] += jnp.dot(quotient, tile, preferred_element_type=F32)
            return carry

        lax.fori_loop(0, tiles, sweep_tile, 0, unroll=2)
        part_out[it] = acc[...].astype(BF)

    def settle(it):
        part_in[it, n - 1] = part_out[it, rows(me), :]
        wait_bytes(part_in.at[it, pl.ds(0, n - 1)], part_r.at[it])
        summed = sum(part_in[it, q].astype(F32) for q in range(n))
        return prior + theta[it, rows(me), :].astype(F32) * summed

    def stats_tile(i, carry):
        cols = tile_columns(i)
        gathered = lax.dot_general(ratio[:, cols], theta[last], (((0,), (0,)), ((), ())),
                                   preferred_element_type=F32)
        weights[cols, :] = jnp.log(beta[cols, :].astype(F32) * gathered + prior_count)
        return carry

    for it in range(last):
        sweep(it)
        send_parts(it)
        theta[it + 1, rows(me), :] = expected_proportions(settle(it)).astype(BF)
        send_theta(it + 1)

    sweep(last)
    own = jnp.sum(theta[last].astype(F32) * acc[...], axis=0, keepdims=True)
    tot_out[...] = jnp.broadcast_to(own, eight)
    peers(lambda m, p: to_docs(tot_out, tot_in.at[m - 1], tot_s.at[0], tot_r.at[0], p).start(),
          n, me)
    send_parts(last)
    lax.fori_loop(0, tiles // 2, stats_tile, 0)
    tot_in[n - 1] = tot_out[...]
    wait_bytes(tot_in.at[pl.ds(0, n - 1)], tot_r.at[0])
    row_out[...] = sum(tot_in[q] for q in range(n))
    peers(lambda m, p: to_tm(row_out, row_in.at[now], row_s.at[0], row_r.at[0], p).start(),
          slices, now)
    lax.fori_loop(tiles // 2, tiles, stats_tile, 0)

    row_in[now] = row_out[...]
    wait_bytes(row_in.at[pl.ds(0, slices - 1)], row_r.at[0])

    chain = chain_ref[...]
    topics = chain.shape[1]
    previous = initial_scale * chain
    gains, factors = [], []
    for t in range(slices):
        totals = row_in[t, 0:1, :]
        noise = obs_ref[...] * (jnp.sum(totals, axis=1, keepdims=True) / (topics * totals))
        predicted = previous + chain
        gain = predicted / (predicted + noise)
        previous = (1.0 - gain) * predicted
        gains.append(gain)
        factors.append(previous / (previous + chain) if t < slices - 1 else jnp.zeros_like(chain))
    share = [None] * slices
    share[-1] = jnp.ones_like(chain)
    for t in range(slices - 2, -1, -1):
        share[t] = (1.0 - factors[t]) + factors[t] * (1.0 - gains[t + 1]) * share[t + 1]

    def mine(per_slice):
        value = per_slice[0]
        for t in range(1, slices):
            value = jnp.where(now == t, per_slice[t], value)
        return value

    gain, factor, left = mine(gains), mine(factors), mine(share)
    all_words = words * n
    offset = jnp.log((row_in[now, 0:1, :] + prior_count * all_words) / all_words)
    keep = 1.0 - gain
    carried = left * keep
    direct = left * gain

    @pl.when(now == 0)
    def _():
        fwd_in[...] = jnp.zeros_like(fwd_in)

    @pl.when(now == slices - 1)
    def _():
        back_in[...] = jnp.zeros_like(back_in)

    pieces = words // chunk

    def piece(i):
        return pl.ds(pl.multiple_of(i * chunk, chunk), chunk)

    def fwd_copy(i):
        return to_tm(fwd_out.at[piece(i), :], fwd_in.at[piece(i), :], fwd_s.at[i], fwd_r.at[i],
                     lax.rem(now + 1, slices))

    def back_copy(i):
        return to_tm(back_out.at[piece(i), :], back_in.at[piece(i), :], back_s.at[i],
                     back_r.at[i], lax.rem(now + slices - 1, slices))

    lag = 3 * (slices - 1 - 2 * now)
    fwd_lag = jnp.maximum(-lag, 0)
    back_lag = jnp.maximum(lag, 0)
    both_lag = jnp.maximum(fwd_lag, back_lag)

    def step(i, carry):
        f, b, s = i - fwd_lag, i - back_lag, i - both_lag

        @pl.when((f >= 0) & (f < pieces))
        def _():
            @pl.when(now > 0)
            def _():
                fwd_copy(f).wait_recv()

            @pl.when(now < slices - 1)
            def _():
                at = piece(f)
                observed = weights[at, :] - offset
                fwd_out[at, :] = (keep * fwd_in[at, :].astype(F32) + gain * observed).astype(BF)
                fwd_copy(f).start()

        @pl.when((b >= 0) & (b < pieces))
        def _():
            @pl.when(now < slices - 1)
            def _():
                back_copy(b).wait_recv()

            @pl.when(now > 0)
            def _():
                at = piece(b)
                observed = weights[at, :] - offset
                back_out[at, :] = (factor * back_in[at, :].astype(F32)
                                   + direct * observed).astype(BF)
                back_copy(b).start()

        @pl.when((s >= 0) & (s < pieces))
        def _():
            at = piece(s)
            smoothed = (carried * fwd_in[at, :].astype(F32)
                        + direct * (weights[at, :] - offset)
                        + factor * back_in[at, :].astype(F32))
            smooth_ref[at, :] = smoothed.astype(BF)
        return carry

    lax.fori_loop(0, pieces + 3 * (slices - 1), step, 0)
    topics_ref[...] = settle(last)

    wait_bytes(stat_in.at[pl.ds(0, n - 1)], stat_s.at[0])
    wait_bytes(ratio.at[others, :], cnt_s.at[0])
    wait_bytes(tot_in.at[pl.ds(0, n - 1)], tot_s.at[0])
    wait_bytes(row_in.at[pl.ds(0, slices - 1)], row_s.at[0])
    for it in range(ITERS_E):
        wait_bytes(theta.at[it, others, :], theta_s.at[it])
        wait_bytes(part_in.at[it, pl.ds(0, n - 1)], part_s.at[it])

    def drain(i, carry):
        @pl.when(now < slices - 1)
        def _():
            fwd_copy(i).wait_send()

        @pl.when(now > 0)
        def _():
            back_copy(i).wait_send()
        return carry

    lax.fori_loop(0, pieces, drain, 0)


def body(counts, topic_means, doc_topics_init, dirichlet_prior, chain_var, obs_noise):
    n = lax.axis_size("docs")
    slices = lax.axis_size("tm")
    docs = counts.shape[1]
    words, topics = topic_means.shape[1:]
    every = docs * n
    word_tile = min(512, words // 2)
    chunk = max(words // 32, 16)
    pieces = words // chunk
    rounds = max(min(4, docs // 16), 1)
    dma = pltpu.SemaphoreType.DMA
    vmem = pl.BlockSpec(memory_space=pltpu.VMEM)
    smoothed, doc_topics = pl.pallas_call(
        functools.partial(round_kernel, n, slices, word_tile, chunk, rounds),
        out_shape=(jax.ShapeDtypeStruct((words, topics), BF),
                   jax.ShapeDtypeStruct((docs, topics), F32)),
        in_specs=[pl.BlockSpec(memory_space=pl.ANY)] + [vmem] * 5,
        out_specs=(vmem, vmem),
        scratch_shapes=[
            pltpu.VMEM((n, docs, words), jnp.int32),
            pltpu.VMEM((n - 1, docs, words), BF),
            pltpu.VMEM((every, words), BF),
            pltpu.VMEM((words, topics), F32),
            pltpu.VMEM((words, topics), BF),
            pltpu.VMEM((ITERS_E, every, topics), BF),
            pltpu.VMEM((every, topics), F32),
            pltpu.VMEM((ITERS_E, every, topics), BF),
            pltpu.VMEM((ITERS_E, n, docs, topics), BF),
            pltpu.VMEM((2, 8, topics), F32),
            pltpu.VMEM((n, 2, 8, topics), F32),
            pltpu.VMEM((8, topics), F32),
            pltpu.VMEM((n, 8, topics), F32),
            pltpu.VMEM((8, topics), F32),
            pltpu.VMEM((slices, 8, topics), F32),
            pltpu.VMEM((words, topics), BF),
            pltpu.VMEM((words, topics), BF),
            pltpu.VMEM((words, topics), BF),
            pltpu.VMEM((words, topics), BF),
            dma((n,)),
            dma((1,)), dma((1,)),
            dma((ITERS_E,)), dma((ITERS_E,)),
            dma((ITERS_E,)), dma((ITERS_E,)),
            dma((1,)), dma((1,)),
            dma((1,)), dma((1,)),
            dma((1,)), dma((1,)),
            dma((pieces,)), dma((pieces,)),
            dma((pieces,)), dma((pieces,)),
        ],
        compiler_params=pltpu.CompilerParams(
            collective_id=0, has_side_effects=True, vmem_limit_bytes=58 * 1024 * 1024),
    )(counts[0], topic_means[0], doc_topics_init[0], dirichlet_prior[None], chain_var[None],
      obs_noise[None])
    return smoothed.astype(F32)[None], doc_topics[None]


def solution(mesh):
    in_specs = (P("tm", "docs", None), P("tm", "docs", None), P("tm", "docs", None), P(), P(), P())
    out_specs = (P("tm", "docs", None), P("tm", "docs", None))
    return jax.shard_map(body, mesh=mesh, in_specs=in_specs, out_specs=out_specs, check_vma=False)
```

```python
import functools

import jax
import jax.numpy as jnp
from jax import lax
from jax.experimental import pallas as pl
from jax.experimental.pallas import tpu as pltpu
from jax.sharding import PartitionSpec as P

ITERS_E = 4
prior_count = 0.5
initial_scale = 1000.0
MESH = pl.DeviceIdType.MESH
BF = jnp.bfloat16
F32 = jnp.float32


def expected_proportions(x):
    u = x * (x + 5.0)
    steps = (2.0 * x + 5.0) * (1.0 / u + 1.0 / (u + 4.0) + 1.0 / (u + 6.0))
    y = x + 6.0
    inv = 1.0 / y
    sq = inv * inv
    tail = sq * (1.0 / 12 - sq * (1.0 / 120 - sq * (1.0 / 252 - sq * (1.0 / 240))))
    return jnp.exp(jnp.log(y) - 0.5 * inv - tail - steps)


def round_kernel(n, slices, word_tile, chunk, rounds, counts_ref, slab_ref, init_ref, prior_ref, chain_ref,
                 obs_ref, smooth_ref, topics_ref, raw, outgoing, ratio, inverse, weights, beta, theta,
                 acc, part_out, part_in, stat_out, stat_in, tot_out, tot_in, row_out, row_in,
                 fwd_in, back_in, fwd_out, back_out, load_sem, cnt_s, cnt_r, theta_s, theta_r,
                 part_s, part_r, stat_s, stat_r, tot_s, tot_r, row_s, row_r, fwd_s, fwd_r,
                 back_s, back_r):
    docs = init_ref.shape[0]
    words = slab_ref.shape[0]
    me = lax.axis_index("docs")
    now = lax.axis_index("tm")

    def peers(fn, size, own):
        for m in range(1, size):
            fn(m, lax.rem(own + m, size))

    def wait_bytes(ref, sem):
        pltpu.make_async_copy(ref, ref, sem).wait()

    def rows(p):
        return pl.ds(pl.multiple_of(p * docs, docs), docs)

    others = pl.ds(0, (n - 1) * docs)

    def load(p):
        return pltpu.make_async_copy(
            counts_ref.at[:, pl.ds(pl.multiple_of(p * words, words), words)], raw.at[p],
            load_sem.at[p])

    def to_docs(src, dst, s, r, p):
        return pltpu.make_async_remote_copy(src_ref=src, dst_ref=dst, send_sem=s, recv_sem=r,
                                            device_id={"docs": p}, device_id_type=MESH)

    def to_tm(src, dst, s, r, p):
        return pltpu.make_async_remote_copy(src_ref=src, dst_ref=dst, send_sem=s, recv_sem=r,
                                            device_id={"tm": p}, device_id_type=MESH)

    def load_all(p, carry):
        load(p).start()
        return carry

    lax.fori_loop(0, n, load_all, 0)

    barrier = pltpu.get_barrier_semaphore()
    peers(lambda m, p: pl.semaphore_signal(barrier, inc=1, device_id={"docs": p},
                                           device_id_type=MESH), n, me)
    peers(lambda m, p: pl.semaphore_signal(barrier, inc=1, device_id={"tm": p},
                                           device_id_type=MESH), slices, now)

    def send_theta(it):
        block = theta.at[it, rows(me), :]
        peers(lambda m, p: to_docs(block, block, theta_s.at[it], theta_r.at[it], p).start(), n, me)

    def send_parts(it):
        peers(lambda m, p: to_docs(part_out.at[it, rows(p), :], part_in.at[it, m - 1],
                                   part_s.at[it], part_r.at[it], p).start(), n, me)

    pl.semaphore_wait(barrier, n - 1 + slices - 1)

    part = docs // rounds

    def send_part(m, r):
        span = pl.ds(pl.multiple_of(r * part, part), part)
        there = pl.ds(pl.multiple_of(me * docs + r * part, part), part)
        to_docs(outgoing.at[m - 1, span, :], ratio.at[there, :], cnt_s.at[0], cnt_r.at[0],
                lax.rem(me + m, n)).start()

    def first_round(m, carry):
        p = lax.rem(me + m, n)
        load(p).wait()
        outgoing[m - 1] = raw[p].astype(F32).astype(BF)
        send_part(m, 0)
        return carry

    lax.fori_loop(1, n, first_round, 0)

    theta[0, rows(me), :] = expected_proportions(init_ref[...]).astype(BF)
    peak = jnp.max(slab_ref[...], axis=0, keepdims=True)
    weights[...] = jnp.exp(slab_ref[...] - peak)
    mass = jnp.sum(weights[...], axis=0, keepdims=True)
    eight = (8, peak.shape[1])
    stat_out[0] = jnp.broadcast_to(peak, eight)
    stat_out[1] = jnp.broadcast_to(mass, eight)
    peers(lambda m, p: to_docs(stat_out, stat_in.at[m - 1], stat_s.at[0], stat_r.at[0], p).start(),
          n, me)
    send_theta(0)

    def later_rounds(i, carry):
        send_part(1 + lax.rem(i, n - 1), 1 + i // (n - 1))
        return carry

    lax.fori_loop(0, (rounds - 1) * (n - 1), later_rounds, 0)
    load(me).wait()
    ratio[rows(me), :] = raw[me].astype(F32).astype(BF)

    stat_in[n - 1] = stat_out[...]
    wait_bytes(stat_in.at[pl.ds(0, n - 1)], stat_r.at[0])
    all_peaks = [stat_in[q, 0, 0:1, :] for q in range(n)]
    top = functools.reduce(jnp.maximum, all_peaks)
    total_mass = sum(stat_in[q, 1, 0:1, :] * jnp.exp(all_peaks[q] - top) for q in range(n))
    beta[...] = (weights[...] * (jnp.exp(peak - top) / total_mass)).astype(BF)

    prior = prior_ref[...]
    last = ITERS_E - 1
    tiles = words // word_tile

    def tile_columns(i):
        return pl.ds(pl.multiple_of(i * word_tile, word_tile), word_tile)

    def sweep(it):
        wait_bytes(theta.at[it, others, :], theta_r.at[it])
        def invert(i):
            mixture = lax.dot_general(theta[it], beta[tile_columns(i), :],
                                      (((1,), (1,)), ((), ())), preferred_element_type=F32)
            guess = pl.reciprocal(mixture, approx=True)
            return (guess * (2.0 - mixture * guess)).astype(BF)

        if it == 0:
            def early(i, carry):
                inverse[:, tile_columns(i)] = invert(i)
                return carry

            lax.fori_loop(0, tiles, early, 0)
            wait_bytes(ratio.at[others, :], cnt_r.at[0])
        acc[...] = jnp.zeros_like(acc)

        def sweep_tile(i, carry):
            cols = tile_columns(i)
            tile = beta[cols, :]
            quotient = ratio[:, cols] * (inverse[:, cols] if it == 0 else invert(i))
            if it == last:
                ratio[:, cols] = quotient
            acc[...] += jnp.dot(quotient, tile, preferred_element_type=F32)
            return carry

        lax.fori_loop(0, tiles, sweep_tile, 0, unroll=2)
        part_out[it] = acc[...].astype(BF)

    def settle(it):
        part_in[it, n - 1] = part_out[it, rows(me), :]
        wait_bytes(part_in.at[it, pl.ds(0, n - 1)], part_r.at[it])
        summed = sum(part_in[it, q].astype(F32) for q in range(n))
        return prior + theta[it, rows(me), :].astype(F32) * summed

    def stats_tile(i, carry):
        cols = tile_columns(i)
        gathered = lax.dot_general(ratio[:, cols], theta[last], (((0,), (0,)), ((), ())),
                                   preferred_element_type=F32)
        weights[cols, :] = jnp.log(beta[cols, :].astype(F32) * gathered + prior_count)
        return carry

    for it in range(last):
        sweep(it)
        send_parts(it)
        theta[it + 1, rows(me), :] = expected_proportions(settle(it)).astype(BF)
        send_theta(it + 1)

    sweep(last)
    own = jnp.sum(theta[last].astype(F32) * acc[...], axis=0, keepdims=True)
    tot_out[...] = jnp.broadcast_to(own, eight)
    peers(lambda m, p: to_docs(tot_out, tot_in.at[m - 1], tot_s.at[0], tot_r.at[0], p).start(),
          n, me)
    send_parts(last)
    lax.fori_loop(0, tiles // 2, stats_tile, 0)
    tot_in[n - 1] = tot_out[...]
    wait_bytes(tot_in.at[pl.ds(0, n - 1)], tot_r.at[0])
    row_out[...] = sum(tot_in[q] for q in range(n))
    peers(lambda m, p: to_tm(row_out, row_in.at[now], row_s.at[0], row_r.at[0], p).start(),
          slices, now)
    lax.fori_loop(tiles // 2, tiles, stats_tile, 0)

    row_in[now] = row_out[...]
    wait_bytes(row_in.at[pl.ds(0, slices - 1)], row_r.at[0])

    chain = chain_ref[...]
    topics = chain.shape[1]
    previous = initial_scale * chain
    gains, factors = [], []
    for t in range(slices):
        totals = row_in[t, 0:1, :]
        noise = obs_ref[...] * (jnp.sum(totals, axis=1, keepdims=True) / (topics * totals))
        predicted = previous + chain
        gain = predicted / (predicted + noise)
        previous = (1.0 - gain) * predicted
        gains.append(gain)
        factors.append(previous / (previous + chain) if t < slices - 1 else jnp.zeros_like(chain))
    share = [None] * slices
    share[-1] = jnp.ones_like(chain)
    for t in range(slices - 2, -1, -1):
        share[t] = (1.0 - factors[t]) + factors[t] * (1.0 - gains[t + 1]) * share[t + 1]

    def mine(per_slice):
        value = per_slice[0]
        for t in range(1, slices):
            value = jnp.where(now == t, per_slice[t], value)
        return value

    gain, factor, left = mine(gains), mine(factors), mine(share)
    all_words = words * n
    offset = jnp.log((row_in[now, 0:1, :] + prior_count * all_words) / all_words)
    keep = 1.0 - gain
    carried = left * keep
    direct = left * gain

    @pl.when(now == 0)
    def _():
        fwd_in[...] = jnp.zeros_like(fwd_in)

    @pl.when(now == slices - 1)
    def _():
        back_in[...] = jnp.zeros_like(back_in)

    pieces = words // chunk

    def piece(i):
        return pl.ds(pl.multiple_of(i * chunk, chunk), chunk)

    def fwd_copy(i):
        return to_tm(fwd_out.at[piece(i), :], fwd_in.at[piece(i), :], fwd_s.at[i], fwd_r.at[i],
                     lax.rem(now + 1, slices))

    def back_copy(i):
        return to_tm(back_out.at[piece(i), :], back_in.at[piece(i), :], back_s.at[i],
                     back_r.at[i], lax.rem(now + slices - 1, slices))

    lag = 2 * (slices - 1 - 2 * now)
    fwd_lag = jnp.maximum(-lag, 0)
    back_lag = jnp.maximum(lag, 0)
    both_lag = jnp.maximum(fwd_lag, back_lag)

    def step(i, carry):
        f, b, s = i - fwd_lag, i - back_lag, i - both_lag

        @pl.when((f >= 0) & (f < pieces))
        def _():
            @pl.when(now > 0)
            def _():
                fwd_copy(f).wait_recv()

            @pl.when(now < slices - 1)
            def _():
                at = piece(f)
                observed = weights[at, :] - offset
                fwd_out[at, :] = (keep * fwd_in[at, :].astype(F32) + gain * observed).astype(BF)
                fwd_copy(f).start()

        @pl.when((b >= 0) & (b < pieces))
        def _():
            @pl.when(now < slices - 1)
            def _():
                back_copy(b).wait_recv()

            @pl.when(now > 0)
            def _():
                at = piece(b)
                observed = weights[at, :] - offset
                back_out[at, :] = (factor * back_in[at, :].astype(F32)
                                   + direct * observed).astype(BF)
                back_copy(b).start()

        @pl.when((s >= 0) & (s < pieces))
        def _():
            at = piece(s)
            smoothed = (carried * fwd_in[at, :].astype(F32)
                        + direct * (weights[at, :] - offset)
                        + factor * back_in[at, :].astype(F32))
            smooth_ref[at, :] = smoothed.astype(BF)
        return carry

    lax.fori_loop(0, pieces + 2 * (slices - 1), step, 0)
    topics_ref[...] = settle(last)

    wait_bytes(stat_in.at[pl.ds(0, n - 1)], stat_s.at[0])
    wait_bytes(ratio.at[others, :], cnt_s.at[0])
    wait_bytes(tot_in.at[pl.ds(0, n - 1)], tot_s.at[0])
    wait_bytes(row_in.at[pl.ds(0, slices - 1)], row_s.at[0])
    for it in range(ITERS_E):
        wait_bytes(theta.at[it, others, :], theta_s.at[it])
        wait_bytes(part_in.at[it, pl.ds(0, n - 1)], part_s.at[it])

    def drain(i, carry):
        @pl.when(now < slices - 1)
        def _():
            fwd_copy(i).wait_send()

        @pl.when(now > 0)
        def _():
            back_copy(i).wait_send()
        return carry

    lax.fori_loop(0, pieces, drain, 0)


def body(counts, topic_means, doc_topics_init, dirichlet_prior, chain_var, obs_noise):
    n = lax.axis_size("docs")
    slices = lax.axis_size("tm")
    docs = counts.shape[1]
    words, topics = topic_means.shape[1:]
    every = docs * n
    word_tile = min(512, words // 2)
    chunk = max(words // 16, 16)
    pieces = words // chunk
    rounds = max(min(4, docs // 16), 1)
    dma = pltpu.SemaphoreType.DMA
    vmem = pl.BlockSpec(memory_space=pltpu.VMEM)
    smoothed, doc_topics = pl.pallas_call(
        functools.partial(round_kernel, n, slices, word_tile, chunk, rounds),
        out_shape=(jax.ShapeDtypeStruct((words, topics), BF),
                   jax.ShapeDtypeStruct((docs, topics), F32)),
        in_specs=[pl.BlockSpec(memory_space=pl.ANY)] + [vmem] * 5,
        out_specs=(vmem, vmem),
        scratch_shapes=[
            pltpu.VMEM((n, docs, words), jnp.int32),
            pltpu.VMEM((n - 1, docs, words), BF),
            pltpu.VMEM((every, words), BF),
            pltpu.VMEM((every, words), BF),
            pltpu.VMEM((words, topics), F32),
            pltpu.VMEM((words, topics), BF),
            pltpu.VMEM((ITERS_E, every, topics), BF),
            pltpu.VMEM((every, topics), F32),
            pltpu.VMEM((ITERS_E, every, topics), BF),
            pltpu.VMEM((ITERS_E, n, docs, topics), BF),
            pltpu.VMEM((2, 8, topics), F32),
            pltpu.VMEM((n, 2, 8, topics), F32),
            pltpu.VMEM((8, topics), F32),
            pltpu.VMEM((n, 8, topics), F32),
            pltpu.VMEM((8, topics), F32),
            pltpu.VMEM((slices, 8, topics), F32),
            pltpu.VMEM((words, topics), BF),
            pltpu.VMEM((words, topics), BF),
            pltpu.VMEM((words, topics), BF),
            pltpu.VMEM((words, topics), BF),
            dma((n,)),
            dma((1,)), dma((1,)),
            dma((ITERS_E,)), dma((ITERS_E,)),
            dma((ITERS_E,)), dma((ITERS_E,)),
            dma((1,)), dma((1,)),
            dma((1,)), dma((1,)),
            dma((1,)), dma((1,)),
            dma((pieces,)), dma((pieces,)),
            dma((pieces,)), dma((pieces,)),
        ],
        compiler_params=pltpu.CompilerParams(
            collective_id=0, has_side_effects=True, vmem_limit_bytes=58 * 1024 * 1024),
    )(counts[0], topic_means[0], doc_topics_init[0], dirichlet_prior[None], chain_var[None],
      obs_noise[None])
    return smoothed.astype(F32)[None], doc_topics[None]


def solution(mesh):
    in_specs = (P("tm", "docs", None), P("tm", "docs", None), P("tm", "docs", None), P(), P(), P())
    out_specs = (P("tm", "docs", None), P("tm", "docs", None))
    return jax.shard_map(body, mesh=mesh, in_specs=in_specs, out_specs=out_specs, check_vma=False)
```
